32 devices in a mesh: groups: 2 (over x), expo: 8 (over z, y), sky: 2 (over core).
Axes of the slice: x: 2, y: 2, z: 4, core: 2. Of those that a mesh axis runs over, the one named last changes fastest.
Arguments:
- exposures: bfloat16 [384, 256, 512], P(('groups', 'expo'), 'sky'), parts along dimension 0, may hold values from -8 to 8
- slot_ids: int32 [16, 24], P('groups'), parts along dimension 0, may hold values from 0 to 128, as said below
- row_range: int32 [256, 2], P('groups'), parts along dimension 0, may hold values from 1 to 256, as said below
- bad_bands: int32 [256, 4], P('groups'), parts along dimension 0, may hold values 0 or 1
- kernel_choice: int32 [256, 4], P('groups'), parts along dimension 0, may hold values from 0 to 9
- flux_scale: float32 [256], P('groups'), parts along dimension 0, may hold values from 0.25 to 4
- vert_taps: bfloat16 [20, 21], P('groups'), parts along dimension 0, may hold values from -0.6 to 1.6
- horiz_taps: bfloat16 [20, 21], P('groups'), parts along dimension 0, may hold values from -0.6 to 1.6
Outputs:
- coadd_plane: float32 [4, 128, 512], P(('groups', 'sky'), 'expo'), parts along dimension 0
- rejected_count: int32 [4, 128, 512], P(('groups', 'sky'), 'expo'), parts along dimension 0
The draws below stay inside these ranges and needn't reach their ends.
There are 2 independent parts, one for each index of `groups`. The reference program is written for one: setup_inputs(seed, part) draws one part's arguments, and reference() takes and returns one part's arrays. A program takes and returns all parts, laid end to end along the dimension named above; each array names one. Nothing has to cross between parts.
Inputs may be any that keep to these rules, and one draw needn't show every extreme that they name: `slot_ids`: each exposure number below 128 stands in exactly one slot; in each row the occupied slots come first and the others hold 128; a row has 8 to 24 occupied slots, and some row has all 24. `row_range`: column 0 is below 128 and column 1 is at least 128 and above column 0.
All inputs are finite; a program needn't handle non-finite values.
Results may differ from the reference program's by a relative error of at most 0.008.
Values may be sent and summed in bfloat16 or wider, within the bound.
No kernel may reach another device: no remote copies, remote signals or barrier semaphores. Data moves between devices by JAX's collectives and lax.ppermute only.
A program may use at most 128 MiB of HBM per device.

```python
import math
import jax
import jax.numpy as jnp
from jax import lax

COLS = 512
BAND_COLS = 128
TAPS = 21
NKERN = 10
REJECT = 4
MIN_VALID = 12
EXP_MEAN = 16
ROW_DEV = 128
SLOTS = 24
EXPOSURES = 128
SLOTS_ALL = 192
NROWS = 256
BANDS = 4
N_EXPO = 8
N_SKY = 2


def draw_exposures(key, part):
    sky_field = jax.random.normal(jax.random.fold_in(key, 1), (NROWS, COLS), jnp.float32)
    jitter = jax.random.normal(jax.random.fold_in(key, 2), (SLOTS_ALL, NROWS, COLS), jnp.float32)
    return jnp.clip(sky_field[None] + jitter, -8.0, 8.0).astype(jnp.bfloat16)


def draw_slot_ids(key, part):
    pair_count = N_EXPO // 2
    half_mean = EXP_MEAN // 2
    imbalance = jax.random.randint(jax.random.fold_in(key, 11), (pair_count,), 0, half_mean + 1)
    imbalance = imbalance.at[0].set(half_mean)
    flipped = jax.random.randint(jax.random.fold_in(key, 12), (pair_count,), 0, 2)
    first_count = EXP_MEAN + imbalance * (1 - 2 * flipped)
    second_count = 2 * EXP_MEAN - first_count
    per_device = jnp.stack([first_count, second_count], 1).reshape(N_EXPO)
    shuffle = jax.random.permutation(jax.random.fold_in(key, 13), N_EXPO)
    per_device = per_device[shuffle]
    offsets = jnp.cumsum(per_device) - per_device
    numbers = jax.random.permutation(jax.random.fold_in(key, 14), EXPOSURES)
    slot_place = jnp.arange(SLOTS)
    position = jnp.clip(offsets[:, None] + slot_place[None, :], 0, EXPOSURES - 1)
    occupied = slot_place[None, :] < per_device[:, None]
    return jnp.where(occupied, numbers[position], EXPOSURES).astype(jnp.int32)


def draw_row_range(key, part):
    early_total = min(20, EXPOSURES // 2)
    strip_rows = NROWS // 8
    ranking = jax.random.permutation(jax.random.fold_in(key, 23), EXPOSURES)
    early = ranking < early_total
    early_first = jax.random.randint(jax.random.fold_in(key, 21), (EXPOSURES,), 1, strip_rows)
    later_first = jax.random.randint(jax.random.fold_in(key, 24), (EXPOSURES,), strip_rows, NROWS // 2)
    first_row = jnp.where(early, early_first, later_first)
    first_row = jnp.where(ranking == 0, 1, first_row)
    extent = jax.random.randint(jax.random.fold_in(key, 22), (EXPOSURES,), NROWS // 2, NROWS + 1)
    last_row = jnp.minimum(first_row + extent, NROWS)
    last_row = jnp.where(ranking == 0, NROWS, last_row)
    return jnp.stack([first_row, last_row], 1).astype(jnp.int32)


def filter_bank(key):
    spread = jnp.clip(0.2 * jax.random.normal(key, (NKERN, TAPS), jnp.float32), -0.55, 0.55)
    centre = (jnp.arange(TAPS) == TAPS // 2).astype(jnp.float32)
    return (spread + centre[None, :]).astype(jnp.bfloat16)


def draw_vert_taps(key, part):
    return filter_bank(jax.random.fold_in(key, 31))


def draw_horiz_taps(key, part):
    return filter_bank(jax.random.fold_in(key, 32))


def plant(drawn, key, least, high):
    spot = [jax.random.randint(jax.random.fold_in(key, axis), (), 0, length) for axis, length in enumerate(drawn.shape)]
    longest = drawn.shape.index(max(drawn.shape))
    beside = spot[:longest] + [(spot[longest] + 1) % drawn.shape[longest]] + spot[longest + 1:]
    return drawn.at[tuple(spot)].set(least).at[tuple(beside)].set(high)


def setup_inputs(seed: int = 0, part: int = 0) -> dict:
    splits = jax.random.split(jax.random.key(seed), 9)
    part_keys = jax.random.split(jax.random.fold_in(splits[8], part), 9)
    return {
        "exposures": draw_exposures(jax.random.fold_in(jax.random.fold_in(splits[8], part), 71), part),
        "slot_ids": draw_slot_ids(jax.random.fold_in(jax.random.fold_in(splits[8], part), 71), part),
        "row_range": draw_row_range(jax.random.fold_in(jax.random.fold_in(splits[8], part), 71), part),
        "bad_bands": plant((jax.random.randint(part_keys[3], (EXPOSURES, BANDS), 0, 8) < 1).astype(jnp.int32), jax.random.fold_in(part_keys[3], 1), 0, 1),
        "kernel_choice": plant(jax.random.randint(part_keys[4], (EXPOSURES, BANDS), 0, NKERN), jax.random.fold_in(part_keys[4], 1), 0, NKERN - 1).astype(jnp.int32),
        "flux_scale": jnp.clip(jnp.exp(jax.random.uniform(part_keys[5], (EXPOSURES,), jnp.float32, math.log(0.25), math.log(4.0))), 0.25, 4.0),
        "vert_taps": draw_vert_taps(jax.random.fold_in(jax.random.fold_in(splits[8], part), 71), part),
        "horiz_taps": draw_horiz_taps(jax.random.fold_in(jax.random.fold_in(splits[8], part), 71), part),
    }


SENTINEL = 1.0e30


def filter_slot(picture, vertical_taps, horizontal_taps):
    margin = TAPS // 2
    band_index = jnp.arange(COLS, dtype=jnp.int32) // BAND_COLS
    column_vertical = vertical_taps[band_index]
    column_horizontal = horizontal_taps[band_index]
    padded = jnp.pad(picture.astype(jnp.float32), ((margin, margin), (0, 0)))
    vertical = jnp.zeros((NROWS, COLS), jnp.float32)
    for offset in range(TAPS):
        vertical = vertical + column_vertical[:, offset][None, :] * padded[offset:offset + NROWS, :]
    rounded = lax.optimization_barrier(vertical.astype(jnp.bfloat16)).astype(jnp.float32)
    widened = jnp.pad(rounded, ((0, 0), (margin, margin)))
    horizontal = jnp.zeros((NROWS, COLS), jnp.float32)
    for offset in range(TAPS):
        horizontal = horizontal + column_horizontal[:, offset][None, :] * widened[:, offset:offset + COLS]
    return horizontal


def one_slot(packed):
    picture, vertical_taps, horizontal_taps, factor = packed
    return (filter_slot(picture, vertical_taps, horizontal_taps) * factor).astype(jnp.bfloat16)


def in_groups(tensor):
    return tensor.reshape((SLOTS_ALL // 8, 8) + tensor.shape[1:])


def reference(exposures, slot_ids, row_range, bad_bands, kernel_choice, flux_scale, vert_taps, horiz_taps):
    slot_list = slot_ids.reshape(-1)
    occupied = slot_list < EXPOSURES
    lookup = jnp.minimum(slot_list, EXPOSURES - 1)
    chosen = kernel_choice[lookup]
    slot_vertical = vert_taps.astype(jnp.float32)[chosen]
    slot_horizontal = horiz_taps.astype(jnp.float32)[chosen]
    slot_scale = flux_scale[lookup]
    planes = lax.map(jax.vmap(one_slot), (in_groups(exposures), in_groups(slot_vertical), in_groups(slot_horizontal), in_groups(slot_scale)))
    planes = planes.reshape(SLOTS_ALL, NROWS, COLS)
    row_index = jnp.arange(NROWS, dtype=jnp.int32)
    row_usable = (row_index[None, :] >= row_range[lookup, 0][:, None]) & (row_index[None, :] < row_range[lookup, 1][:, None]) & occupied[:, None]
    band_index = jnp.arange(COLS, dtype=jnp.int32) // BAND_COLS
    column_usable = (bad_bands[lookup] == 0)[:, band_index]

    def one_row(row_number):
        values = lax.dynamic_index_in_dim(planes, row_number, 1, keepdims=False).astype(jnp.float32)
        usable = lax.dynamic_index_in_dim(row_usable, row_number, 1, keepdims=False)[:, None] & column_usable
        cover_count = jnp.sum(usable.astype(jnp.int32), axis=0, dtype=jnp.int32)
        grand_total = jnp.sum(jnp.where(usable, values, 0.0), axis=0)
        highest = lax.top_k(jnp.where(usable, values, -SENTINEL).T, REJECT)[0]
        lowest = lax.top_k(jnp.where(usable, -values, -SENTINEL).T, REJECT)[0]
        top_sum = jnp.sum(highest, axis=1)
        bottom_sum = -jnp.sum(lowest, axis=1)
        clipped = cover_count >= MIN_VALID
        used_count = jnp.where(clipped, cover_count - 2 * REJECT, cover_count)
        kept_sum = jnp.where(clipped, grand_total - top_sum - bottom_sum, grand_total)
        coadd_rows = kept_sum / jnp.maximum(used_count, 1).astype(jnp.float32)
        return coadd_rows, (EXPOSURES - used_count).astype(jnp.int32)

    coadd_plane, rejected_count = lax.map(one_row, row_index)
    return coadd_plane.reshape(N_SKY, ROW_DEV, COLS), rejected_count.reshape(N_SKY, ROW_DEV, COLS)
```

```python
import functools

import jax
import jax.numpy as jnp
from jax import lax
from jax.experimental import pallas as pl
from jax.experimental.pallas import tpu as pltpu
from jax.sharding import PartitionSpec as P

BAND_COLS = 128
TAPS = 21
REJECT = 4
MIN_VALID = 12

SENTINEL = 1e30
HIGHEST = lax.Precision.HIGHEST

TILE_ROWS = 16
PAD = 16
SQUARE = 4
LISTS = 2 * REJECT + 1


def sort_pair(entries, first, second, up):
    a, b = entries[first], entries[second]
    hi, lo = jnp.maximum(a, b), jnp.minimum(a, b)
    entries[first], entries[second] = (hi, lo) if up else (lo, hi)


def sorted_four(entries, up):
    entries = list(entries)
    for first, second in ((0, 1), (2, 3), (0, 2), (1, 3), (1, 2)):
        sort_pair(entries, first, second, up)
    return entries


def merged_four(left, right, up, ordered=True):
    pick = jnp.maximum if up else jnp.minimum
    entries = [pick(left[i], right[REJECT - 1 - i]) for i in range(REJECT)]
    if ordered:
        for first, second in ((0, 2), (1, 3), (0, 1), (2, 3)):
            sort_pair(entries, first, second, up)
    return entries


def valid_sum(highs, lows):
    total = None
    for value in highs + lows:
        wide = value.astype(jnp.float32)
        wide = jnp.where(jnp.abs(wide) < 0.5 * SENTINEL, wide, 0.0)
        total = wide if total is None else total + wide
    return total


def block_kernel(
    slots,
    bands,
    kernels,
    exposures_total,
    rows,
    order_ref,
    table_ref,
    flux_ref,
    slot_ref,
    vert_ref,
    horiz_ref,
    exposures_ref,
    halo_ref,
    *rest,
):
    outs = rest[: rows // TILE_ROWS]
    pictures, high, low, total, bank_v, bank_h, padded, sems = rest[rows // TILE_ROWS :]
    margin = TAPS // 2
    high_rows = rows + 2 * PAD
    chunks = rows // TILE_ROWS
    half = order_ref[0]
    place = order_ref[1]
    sky_place = order_ref[2]
    use_halo = order_ref[3]
    group = 4
    row_dev = exposures_ref.shape[1]
    last = row_dev // rows - 1
    body_rows = rows + PAD
    start = pl.multiple_of(half * (row_dev - body_rows), TILE_ROWS)
    land = pl.multiple_of(PAD - PAD * half, TILE_ROWS)
    edge = pl.multiple_of(half * body_rows, TILE_ROWS)

    def body_copy(piece):
        return pltpu.make_async_copy(
            exposures_ref.at[pl.ds(piece * group, group), pl.ds(start, body_rows), :],
            pictures.at[pl.ds(piece * group, group), pl.ds(land, body_rows), :],
            sems.at[piece],
        )

    pieces = slots // group
    halo_copy = pltpu.make_async_copy(
        halo_ref, pictures.at[:, pl.ds(edge, PAD), :], sems.at[pieces]
    )
    halo_copy.start()
    for piece in range(pieces):
        body_copy(piece).start()

    padded[...] = jnp.zeros_like(padded)
    padded[0, :kernels, :TAPS] = vert_ref[...].astype(jnp.float32)
    padded[1, :kernels, :TAPS] = horiz_ref[...].astype(jnp.float32)
    vert_lines = pltpu.roll(padded[0], PAD - margin, 1)
    horiz_lines = pltpu.roll(padded[1], BAND_COLS - margin, 1)
    offset = lax.broadcasted_iota(jnp.int32, (BAND_COLS, BAND_COLS), 1) - (
        lax.broadcasted_iota(jnp.int32, (BAND_COLS, BAND_COLS), 0)
    )
    inside = jnp.abs(offset) < BAND_COLS // 2
    for kernel in range(kernels):
        line = jnp.broadcast_to(vert_lines[kernel : kernel + 1], (rows, BAND_COLS))
        banded = pltpu.roll(line, 0, 1, stride=1, stride_axis=0)
        bank_v[kernel] = banded[:, :high_rows].astype(jnp.bfloat16)
        line = jnp.broadcast_to(horiz_lines[kernel : kernel + 1], (BAND_COLS, BAND_COLS))
        banded = pltpu.roll(line, 0, 1, stride=1, stride_axis=0)
        bank_h[kernel, :BAND_COLS] = jnp.where(inside, banded, 0.0).T.astype(jnp.bfloat16)
        bank_h[kernel, BAND_COLS:] = jnp.where(inside, 0.0, banded).T.astype(jnp.bfloat16)

    total[...] = jnp.zeros_like(total)
    halo_copy.wait()

    @pl.when(use_halo == 0)
    def _():
        pictures[:, pl.ds(edge, PAD), :] = jnp.zeros_like(halo_ref)

    first_row = sky_place * row_dev + half * rows
    row_index = first_row + lax.broadcasted_iota(jnp.int32, (rows, BAND_COLS), 0)
    lane = lax.broadcasted_iota(jnp.int32, (rows, BAND_COLS), 1)

    def one_slot(slot):
        ident = slot_ref[place, slot]
        occupied = ident < exposures_total
        k = jnp.minimum(ident, exposures_total - 1)
        span = table_ref[bands, k]
        begin = lax.rem(span, 65536)
        end = jnp.where(occupied, lax.div(span, 65536), 0)
        factor = flux_ref[k]
        codes = [table_ref[band, k] for band in range(bands)]
        chosen = [lax.rem(code, 65536) for code in codes]
        columns = []
        for band in range(bands):
            picture = pictures[slot, :, band * BAND_COLS : (band + 1) * BAND_COLS]
            vertical = jnp.dot(
                bank_v[chosen[band]], picture, preferred_element_type=jnp.float32
            )
            columns.append(vertical.astype(jnp.bfloat16))
        nothing = jnp.zeros_like(columns[0])
        for band in range(bands):
            before = columns[band - 1] if band else nothing
            after = columns[band + 1] if band + 1 < bands else nothing
            sides = jnp.where(lane < BAND_COLS // 2, after, before)
            filtered = jnp.dot(
                jnp.concatenate([columns[band], sides], 1),
                bank_h[chosen[band]],
                preferred_element_type=jnp.float32,
            )
            plane = (filtered * factor).astype(jnp.bfloat16).astype(jnp.float32)
            stop = jnp.where(codes[band] >= 65536, 0, end)
            usable = (row_index >= begin) & (row_index < stop)
            window = pl.ds(band * BAND_COLS, BAND_COLS)
            total[:, window] += jnp.where(usable, plane, 0.0)
            high[slot, :, window] = jnp.where(usable, plane, -SENTINEL).astype(jnp.bfloat16)
            low[slot, :, window] = jnp.where(usable, plane, SENTINEL).astype(jnp.bfloat16)

    for piece in range(pieces):
        body_copy(piece).wait()

        def body(step, carry):
            one_slot(piece * group + 2 * step)
            one_slot(piece * group + 2 * step + 1)
            return carry

        lax.fori_loop(0, group // 2, body, 0)

    for position, out in enumerate(outs):
        top = pl.multiple_of(order_ref[4 + position] * TILE_ROWS, TILE_ROWS)

        def tile(step, carry):
            window = pl.ds(pl.multiple_of(step * BAND_COLS, BAND_COLS), BAND_COLS)
            sides = []
            for source, up in ((high, True), (low, False)):
                best = None
                for piece in range(slots // REJECT):
                    entries = [
                        source[piece * REJECT + i, pl.ds(top, TILE_ROWS), window]
                        for i in range(REJECT)
                    ]
                    entries = sorted_four(entries, up)
                    best = entries if best is None else merged_four(best, entries, up)
                sides.append(best)
            left = total[pl.ds(top, TILE_ROWS), window] - valid_sum(*sides)
            for index, value in enumerate(sides[0] + sides[1]):
                out[index, :, window] = value
            out[2 * REJECT, :, window] = left.astype(jnp.bfloat16)
            return carry

        lax.fori_loop(0, bands, tile, 0)


def filter_block(order, table, flux, slot_ids, vert, horiz, exposures, halo, rows):
    slots, row_dev, columns = exposures.shape
    kernels = vert.shape[0]
    bands = columns // BAND_COLS
    chunks = rows // TILE_ROWS
    smem = pl.BlockSpec(memory_space=pltpu.SMEM)
    vmem = pl.BlockSpec(memory_space=pltpu.VMEM)
    anywhere = pl.BlockSpec(memory_space=pl.ANY)
    body = functools.partial(block_kernel, slots, bands, kernels, flux.shape[0], rows)
    kernel_rows = -(-kernels // 8) * 8
    return pl.pallas_call(
        body,
        out_shape=[jax.ShapeDtypeStruct((LISTS, TILE_ROWS, columns), jnp.bfloat16)] * chunks,
        in_specs=[smem, smem, smem, smem, vmem, vmem, anywhere, anywhere],
        out_specs=[vmem] * chunks,
        scratch_shapes=[
            pltpu.VMEM((slots, rows + 2 * PAD, columns), jnp.bfloat16),
            pltpu.VMEM((slots, rows, columns), jnp.bfloat16),
            pltpu.VMEM((slots, rows, columns), jnp.bfloat16),
            pltpu.VMEM((rows, columns), jnp.float32),
            pltpu.VMEM((kernels, rows, rows + 2 * PAD), jnp.bfloat16),
            pltpu.VMEM((kernels, 2 * BAND_COLS, BAND_COLS), jnp.bfloat16),
            pltpu.VMEM((2, kernel_rows, BAND_COLS), jnp.float32),
            pltpu.SemaphoreType.DMA((slots // 4 + 1,)),
        ],
        compiler_params=pltpu.CompilerParams(vmem_limit_bytes=32 * 1024 * 1024),
        cost_estimate=pl.CostEstimate(
            flops=4 * slots * rows * columns * 256, bytes_accessed=8 << 20, transcendentals=0
        ),
        name="filter_block",
    )(order, table, flux, slot_ids, vert, horiz, exposures, halo)


def merged_lists(refs, window, ordered):
    sides = []
    for base, up in ((0, True), (REJECT, False)):
        lists = [[ref[base + i, :, window] for i in range(REJECT)] for ref in refs]
        while len(lists) > 1:
            keep = ordered or len(lists) > 2
            paired = [
                merged_four(lists[i], lists[i + 1], up, keep)
                for i in range(0, len(lists) - 1, 2)
            ]
            lists = paired + (lists[-1:] if len(lists) % 2 else [])
        sides.append(lists[0])
    grand = None
    for ref in refs:
        part = ref[2 * REJECT, :, window].astype(jnp.float32) + valid_sum(
            [ref[i, :, window] for i in range(REJECT)],
            [ref[REJECT + i, :, window] for i in range(REJECT)],
        )
        grand = part if grand is None else grand + part
    return sides, grand


def merge_kernel(*refs):
    *sources, out = refs
    for band in range(out.shape[-1] // BAND_COLS):
        window = pl.ds(band * BAND_COLS, BAND_COLS)
        sides, grand = merged_lists(sources, window, True)
        for index, value in enumerate(sides[0] + sides[1]):
            out[index, :, window] = value
        out[2 * REJECT, :, window] = (grand - valid_sum(*sides)).astype(jnp.bfloat16)


def merge(parts):
    vmem = pl.BlockSpec(memory_space=pltpu.VMEM)
    return pl.pallas_call(
        merge_kernel,
        out_shape=jax.ShapeDtypeStruct(parts[0].shape, jnp.bfloat16),
        in_specs=[vmem] * len(parts),
        out_specs=vmem,
        name="merge_lists",
    )(*parts)


def finish_kernel(exposures_total, *refs):
    *sources, count_ref, coadd_ref, rejected_ref = refs
    for band in range(coadd_ref.shape[-1] // BAND_COLS):
        window = pl.ds(band * BAND_COLS, BAND_COLS)
        sides, grand = merged_lists(sources, window, False)
        extremes = valid_sum(*sides)
        count = count_ref[:, window]
        clipped = count >= MIN_VALID
        used = jnp.where(clipped, count - 2 * REJECT, count)
        kept = jnp.where(clipped, grand - extremes, grand)
        coadd_ref[:, window] = kept / jnp.maximum(used, 1).astype(jnp.float32)
        rejected_ref[:, window] = exposures_total - used


def finish(parts, count, exposures_total):
    vmem = pl.BlockSpec(memory_space=pltpu.VMEM)
    return pl.pallas_call(
        functools.partial(finish_kernel, exposures_total),
        out_shape=[
            jax.ShapeDtypeStruct(count.shape, jnp.float32),
            jax.ShapeDtypeStruct(count.shape, jnp.int32),
        ],
        in_specs=[vmem] * (len(parts) + 1),
        out_specs=[vmem, vmem],
        name="finish_pixels",
    )(*parts, count)


def usable_count(first_row, row_count, row_range, bad_bands):
    row_place = (first_row + jnp.arange(row_count, dtype=jnp.int32)).astype(jnp.float32)
    bounds = row_range.astype(jnp.float32)
    covered = (
        (row_place[None, :] >= bounds[:, 0:1]) & (row_place[None, :] < bounds[:, 1:2])
    ).astype(jnp.float32)
    clean = (bad_bands == 0).astype(jnp.float32)
    per_band = jnp.dot(covered.T, clean, precision=HIGHEST)
    return jnp.repeat(per_band, BAND_COLS, axis=1).astype(jnp.int32)


def swapped(value, axis, distance):
    count = lax.axis_size(axis)
    return lax.ppermute(value, axis, [(i, i ^ distance) for i in range(count)])


def shards(
    exposures, slot_ids, row_range, bad_bands, kernel_choice, flux_scale, vert_taps, horiz_taps
):
    slot_count, row_dev, columns = exposures.shape
    exposures_total = flux_scale.shape[0]
    expo_size = lax.axis_size("expo")
    expo_place = lax.axis_index("expo")
    sky_place = lax.axis_index("sky")
    rows = row_dev // 2
    rows_out = row_dev // expo_size
    chunks = rows // TILE_ROWS

    edge_rows = lax.dynamic_slice_in_dim(exposures, (1 - sky_place) * (row_dev - PAD), PAD, 1)
    halo = swapped(edge_rows, "sky", 1)

    table = jnp.concatenate(
        [
            kernel_choice + 65536 * (bad_bands != 0).astype(jnp.int32),
            row_range[:, 0:1] + 65536 * row_range[:, 1:2],
        ],
        1,
    ).T

    def block(half, chunk_order):
        order = jnp.stack(
            [half, expo_place, sky_place, (half != sky_place).astype(jnp.int32)] + chunk_order
        ).astype(jnp.int32)
        return filter_block(
            order, table, flux_scale, slot_ids, vert_taps, horiz_taps, exposures, halo, rows
        )

    first_row = sky_place * row_dev + expo_place * rows_out
    count = usable_count(first_row, rows_out, row_range, bad_bands)

    if rows_out == TILE_ROWS and expo_size == 2 * SQUARE:
        near = lax.div(expo_place, SQUARE)
        corner = lax.rem(expo_place, SQUARE)
        chunk_order = [corner ^ distance for distance in range(SQUARE)]
        far_own, *far_sent = block(1 - near, chunk_order)
        far_got = [swapped(part, "expo", 1 + i) for i, part in enumerate(far_sent)]
        near_own, *near_sent = block(near, chunk_order)
        near_got = [swapped(part, "expo", 1 + i) for i, part in enumerate(near_sent)]
        across = swapped(merge([far_own] + far_got), "expo", SQUARE)
        coadd_plane, rejected_count = finish(
            [near_own] + near_got + [across], count, exposures_total
        )
    else:
        natural = [jnp.int32(chunk) for chunk in range(chunks)]
        blocks = block(jnp.int32(0), natural) + block(jnp.int32(1), natural)
        whole = jnp.concatenate(blocks, 1)
        arrived = lax.all_to_all(whole, "expo", split_axis=1, concat_axis=0, tiled=True)
        arrived = arrived.reshape(expo_size, LISTS, rows_out, columns)
        coadd_plane, rejected_count = finish(
            [arrived[i] for i in range(expo_size)], count, exposures_total
        )
    return (coadd_plane[None], rejected_count[None])


def solution(mesh):
    in_specs = (
        P(("groups", "expo"), "sky", None),
        P("groups", None),
        P("groups", None),
        P("groups", None),
        P("groups", None),
        P("groups"),
        P("groups", None),
        P("groups", None),
    )
    out_specs = (P(("groups", "sky"), "expo", None), P(("groups", "sky"), "expo", None))
    return jax.shard_map(shards, mesh=mesh, in_specs=in_specs, out_specs=out_specs, check_vma=False)
```

```python
import functools

import jax
import jax.numpy as jnp
from jax import lax
from jax.experimental import pallas as pl
from jax.experimental.pallas import tpu as pltpu
from jax.sharding import PartitionSpec as P

BAND_COLS = 128
TAPS = 21
REJECT = 4
MIN_VALID = 12

SENTINEL = 1e30

TILE_ROWS = 16
PAD = 16
SQUARE = 4
KERNEL_VMEM = 8 * 1024 * 1024
LISTS = 2 * REJECT + 1


def sort_pair(entries, first, second, up):
    a, b = entries[first], entries[second]
    hi, lo = jnp.maximum(a, b), jnp.minimum(a, b)
    entries[first], entries[second] = (hi, lo) if up else (lo, hi)


def sorted_four(entries, up):
    entries = list(entries)
    for first, second in ((0, 1), (2, 3), (0, 2), (1, 3), (1, 2)):
        sort_pair(entries, first, second, up)
    return entries


def merged_four(left, right, up, ordered=True):
    pick = jnp.maximum if up else jnp.minimum
    entries = [pick(left[i], right[REJECT - 1 - i]) for i in range(REJECT)]
    if ordered:
        for first, second in ((0, 2), (1, 3), (0, 1), (2, 3)):
            sort_pair(entries, first, second, up)
    return entries


def valid_sum(highs, lows):
    total = None
    for value in highs + lows:
        wide = value.astype(jnp.float32)
        wide = jnp.where(jnp.abs(wide) < 0.5 * SENTINEL, wide, 0.0)
        total = wide if total is None else total + wide
    return total


def banded_pair(line):
    offset = lax.broadcasted_iota(jnp.int32, (BAND_COLS, BAND_COLS), 1) - (
        lax.broadcasted_iota(jnp.int32, (BAND_COLS, BAND_COLS), 0)
    )
    inside = jnp.abs(offset) < BAND_COLS // 2
    banded = pltpu.roll(
        jnp.broadcast_to(line, (BAND_COLS, BAND_COLS)), 0, 1, stride=1, stride_axis=0
    )
    return jnp.where(inside, banded, 0.0), jnp.where(inside, 0.0, banded)


def block_kernel(
    slots,
    bands,
    kernels,
    exposures_total,
    rows_out,
    chunk_of,
    exposures_ref,
    halo_ref,
    slot_hbm,
    choice_hbm,
    bad_hbm,
    range_hbm,
    flux_hbm,
    vert_hbm,
    horiz_hbm,
    *rest,
):
    rows = exposures_ref.shape[1]
    chunks = rows // TILE_ROWS
    outs, count_ref, rest = rest[:chunks], rest[chunks], rest[chunks + 1 :]
    (
        pictures,
        high,
        low,
        total,
        bank_v,
        bank_h,
        taps,
        bad_vec,
        range_vec,
        slot_ref,
        choice_ref,
        bad_ref,
        range_ref,
        flux_ref,
        sems,
        halo_sem,
        table_sems,
    ) = rest
    margin = TAPS // 2
    group = 4
    pieces = slots // group
    place = lax.axis_index("expo")
    sky_place = lax.axis_index("sky")

    tables = [
        pltpu.make_async_copy(source, target, table_sems.at[i])
        for i, (source, target) in enumerate(
            (
                (vert_hbm, taps.at[0]),
                (horiz_hbm, taps.at[1]),
                (slot_hbm, slot_ref),
                (choice_hbm, choice_ref),
                (bad_hbm, bad_ref),
                (range_hbm, range_ref),
                (flux_hbm, flux_ref),
                (bad_hbm, bad_vec),
                (range_hbm, range_vec),
            )
        )
    ]
    for copy in tables:
        copy.start()

    def body_copy(piece):
        return pltpu.make_async_copy(
            exposures_ref.at[pl.ds(piece * group, group)],
            pictures.at[pl.ds(piece * group, group), pl.ds(0, rows), :],
            sems.at[piece],
        )

    spot = pl.multiple_of(rows + PAD * (1 - sky_place), TILE_ROWS)
    bare = pl.multiple_of(rows + PAD * sky_place, TILE_ROWS)
    halo_copy = pltpu.make_async_copy(halo_ref, pictures.at[:, pl.ds(spot, PAD), :], halo_sem)
    halo_copy.start()
    for piece in range(pieces):
        body_copy(piece).start()
    pictures[:, pl.ds(bare, PAD), :] = jnp.zeros((slots, PAD, pictures.shape[2]), jnp.bfloat16)
    total[...] = jnp.zeros_like(total)

    tables[0].wait()
    tables[1].wait()
    wide = ((0, 0), (0, BAND_COLS - TAPS))
    vert_lines = jnp.pad(taps[0].astype(jnp.float32), wide)
    vert_lines = pltpu.roll(vert_lines, BAND_COLS - margin, 1)
    horiz_lines = jnp.pad(taps[1].astype(jnp.float32), wide)
    horiz_lines = pltpu.roll(horiz_lines, BAND_COLS - margin, 1)
    for kernel in range(kernels):
        main, edge = banded_pair(vert_lines[kernel : kernel + 1])
        bank_v[kernel, :, :BAND_COLS] = main.astype(jnp.bfloat16)
        bank_v[kernel, :, BAND_COLS:] = pltpu.roll(edge, PAD, 1)[:, : 2 * PAD].astype(jnp.bfloat16)
        main, edge = banded_pair(horiz_lines[kernel : kernel + 1])
        bank_h[kernel, :BAND_COLS] = main.T.astype(jnp.bfloat16)
        bank_h[kernel, BAND_COLS:] = edge.T.astype(jnp.bfloat16)
    for copy in tables[2:]:
        copy.wait()

    first_out = sky_place * rows + place * rows_out
    out_row = first_out + lax.broadcasted_iota(jnp.int32, (rows_out, exposures_total), 0)
    covered = (out_row >= range_vec[0:1, :]) & (out_row < range_vec[1:2, :])
    for band in range(bands):
        both = covered & (bad_vec[band : band + 1, :] == 0)
        number = jnp.sum(both.astype(jnp.float32), axis=1, keepdims=True)
        count_ref[:, band * BAND_COLS : (band + 1) * BAND_COLS] = jnp.broadcast_to(
            number.astype(jnp.int32), (rows_out, BAND_COLS)
        )

    row_index = sky_place * rows + lax.broadcasted_iota(jnp.int32, (rows, BAND_COLS), 0)
    lane = lax.broadcasted_iota(jnp.int32, (rows, BAND_COLS), 1)
    nothing = jnp.zeros((rows, BAND_COLS), jnp.bfloat16)

    def one_slot(slot):
        ident = slot_ref[place, slot]
        k = jnp.minimum(ident, exposures_total - 1)
        begin = range_ref[0, k]
        end = jnp.where(ident < exposures_total, range_ref[1, k], 0)
        factor = flux_ref[k]
        chosen = [choice_ref[band, k] for band in range(bands)]
        columns = []
        for band in range(bands):
            picture = pictures[slot, :, band * BAND_COLS : (band + 1) * BAND_COLS]
            vertical = jnp.dot(bank_v[chosen[band]], picture, preferred_element_type=jnp.float32)
            columns.append(vertical.astype(jnp.bfloat16))
        for band in range(bands):
            before = columns[band - 1] if band else nothing
            after = columns[band + 1] if band + 1 < bands else nothing
            sides = jnp.where(lane < BAND_COLS // 2, after, before)
            filtered = jnp.dot(
                jnp.concatenate([columns[band], sides], 1),
                bank_h[chosen[band]],
                preferred_element_type=jnp.float32,
            )
            plane = (filtered * factor).astype(jnp.bfloat16).astype(jnp.float32)
            stop = jnp.where(bad_ref[band, k] == 0, end, 0)
            usable = (row_index >= begin) & (row_index < stop)
            window = pl.ds(band * BAND_COLS, BAND_COLS)
            total[:, window] += jnp.where(usable, plane, 0.0)
            high[slot, :, window] = jnp.where(usable, plane, -SENTINEL).astype(jnp.bfloat16)
            low[slot, :, window] = jnp.where(usable, plane, SENTINEL).astype(jnp.bfloat16)

    halo_copy.wait()
    for piece in range(pieces):
        body_copy(piece).wait()

        def body(step, carry):
            one_slot(piece * group + 2 * step)
            one_slot(piece * group + 2 * step + 1)
            return carry

        lax.fori_loop(0, group // 2, body, 0)

    for position, out in enumerate(outs):
        top = pl.multiple_of(chunk_of(place, position) * TILE_ROWS, TILE_ROWS)

        def tiles(step, carry):
            for part in range(2):
                window = pl.ds(
                    pl.multiple_of((2 * step + part) * BAND_COLS, BAND_COLS), BAND_COLS
                )
                sides = []
                for source, up in ((high, True), (low, False)):
                    best = None
                    for piece in range(slots // REJECT):
                        entries = [
                            source[piece * REJECT + i, pl.ds(top, TILE_ROWS), window]
                            for i in range(REJECT)
                        ]
                        entries = sorted_four(entries, up)
                        best = entries if best is None else merged_four(best, entries, up)
                    sides.append(best)
                left = total[pl.ds(top, TILE_ROWS), window] - valid_sum(*sides)
                for index, value in enumerate(sides[0] + sides[1]):
                    out[index, :, window] = value
                out[2 * REJECT, :, window] = left.astype(jnp.bfloat16)
            return carry

        lax.fori_loop(0, bands // 2, tiles, 0)


def filter_block(chunk_of, rows_out, exposures, halo, slot_ids, choice, bad, span, flux, vert, horiz):
    slots, rows, columns = exposures.shape
    kernels = vert.shape[0]
    bands = columns // BAND_COLS
    chunks = rows // TILE_ROWS
    hbm = pl.BlockSpec(memory_space=pltpu.HBM)
    vmem = pl.BlockSpec(memory_space=pltpu.VMEM)
    anywhere = pl.BlockSpec(memory_space=pl.ANY)
    body = functools.partial(
        block_kernel, slots, bands, kernels, flux.shape[0], rows_out, chunk_of
    )
    return pl.pallas_call(
        body,
        out_shape=[jax.ShapeDtypeStruct((LISTS, TILE_ROWS, columns), jnp.bfloat16)] * chunks
        + [jax.ShapeDtypeStruct((rows_out, columns), jnp.int32)],
        in_specs=[hbm, anywhere] + [hbm] * 7,
        out_specs=[vmem] * (chunks + 1),
        scratch_shapes=[
            pltpu.VMEM((slots, rows + 2 * PAD, columns), jnp.bfloat16),
            pltpu.VMEM((slots, rows, columns), jnp.bfloat16),
            pltpu.VMEM((slots, rows, columns), jnp.bfloat16),
            pltpu.VMEM((rows, columns), jnp.float32),
            pltpu.VMEM((kernels, rows, BAND_COLS + 2 * PAD), jnp.bfloat16),
            pltpu.VMEM((kernels, 2 * BAND_COLS, BAND_COLS), jnp.bfloat16),
            pltpu.VMEM((2,) + vert.shape, jnp.bfloat16),
            pltpu.VMEM(bad.shape, jnp.int32),
            pltpu.VMEM(span.shape, jnp.int32),
            pltpu.SMEM(slot_ids.shape, jnp.int32),
            pltpu.SMEM(choice.shape, jnp.int32),
            pltpu.SMEM(bad.shape, jnp.int32),
            pltpu.SMEM(span.shape, jnp.int32),
            pltpu.SMEM(flux.shape, jnp.float32),
            pltpu.SemaphoreType.DMA((slots // 4,)),
            pltpu.SemaphoreType.DMA,
            pltpu.SemaphoreType.DMA((9,)),
        ],
        compiler_params=pltpu.CompilerParams(vmem_limit_bytes=40 * 1024 * 1024),
        cost_estimate=pl.CostEstimate(
            flops=4 * slots * rows * columns * 256, bytes_accessed=8 << 20, transcendentals=0
        ),
        name="filter_block",
    )(exposures, halo, slot_ids, choice, bad, span, flux, vert, horiz)


def merged_lists(refs, window, ordered):
    sides = []
    for base, up in ((0, True), (REJECT, False)):
        lists = [[ref[base + i, :, window] for i in range(REJECT)] for ref in refs]
        while len(lists) > 1:
            keep = ordered or len(lists) > 2
            paired = [
                merged_four(lists[i], lists[i + 1], up, keep)
                for i in range(0, len(lists) - 1, 2)
            ]
            lists = paired + (lists[-1:] if len(lists) % 2 else [])
        sides.append(lists[0])
    grand = None
    for ref in refs:
        part = ref[2 * REJECT, :, window].astype(jnp.float32) + valid_sum(
            [ref[i, :, window] for i in range(REJECT)],
            [ref[REJECT + i, :, window] for i in range(REJECT)],
        )
        grand = part if grand is None else grand + part
    return sides, grand


def merge_kernel(*refs):
    *sources, out = refs
    for band in range(out.shape[-1] // BAND_COLS):
        window = pl.ds(band * BAND_COLS, BAND_COLS)
        sides, grand = merged_lists(sources, window, True)
        for index, value in enumerate(sides[0] + sides[1]):
            out[index, :, window] = value
        out[2 * REJECT, :, window] = (grand - valid_sum(*sides)).astype(jnp.bfloat16)


def merge(parts):
    vmem = pl.BlockSpec(memory_space=pltpu.VMEM)
    return pl.pallas_call(
        merge_kernel,
        out_shape=jax.ShapeDtypeStruct(parts[0].shape, jnp.bfloat16),
        in_specs=[vmem] * len(parts),
        out_specs=vmem,
        compiler_params=pltpu.CompilerParams(vmem_limit_bytes=KERNEL_VMEM),
        name="merge_lists",
    )(*parts)


def finish_kernel(exposures_total, *refs):
    *sources, count_ref, coadd_ref, rejected_ref = refs
    for band in range(coadd_ref.shape[-1] // BAND_COLS):
        window = pl.ds(band * BAND_COLS, BAND_COLS)
        sides, grand = merged_lists(sources, window, False)
        extremes = valid_sum(*sides)
        count = count_ref[:, window]
        clipped = count >= MIN_VALID
        used = jnp.where(clipped, count - 2 * REJECT, count)
        kept = jnp.where(clipped, grand - extremes, grand)
        coadd_ref[:, window] = kept / jnp.maximum(used, 1).astype(jnp.float32)
        rejected_ref[:, window] = exposures_total - used


def finish(parts, count, exposures_total):
    vmem = pl.BlockSpec(memory_space=pltpu.VMEM)
    return pl.pallas_call(
        functools.partial(finish_kernel, exposures_total),
        out_shape=[
            jax.ShapeDtypeStruct(count.shape, jnp.float32),
            jax.ShapeDtypeStruct(count.shape, jnp.int32),
        ],
        in_specs=[vmem] * (len(parts) + 1),
        out_specs=[vmem, vmem],
        compiler_params=pltpu.CompilerParams(vmem_limit_bytes=KERNEL_VMEM),
        name="finish_pixels",
    )(*parts, count)


def swapped(value, axis, distance):
    count = lax.axis_size(axis)
    return lax.ppermute(value, axis, [(i, i ^ distance) for i in range(count)])


def shards(
    exposures, slot_ids, row_range, bad_bands, kernel_choice, flux_scale, vert_taps, horiz_taps
):
    slot_count, row_dev, columns = exposures.shape
    exposures_total = flux_scale.shape[0]
    expo_size = lax.axis_size("expo")
    sky_place = lax.axis_index("sky")
    rows_out = row_dev // expo_size

    edge_rows = lax.dynamic_slice_in_dim(exposures, (1 - sky_place) * (row_dev - PAD), PAD, 1)
    halo = swapped(edge_rows, "sky", 1)

    def block(chunk_of):
        *lists, count = filter_block(
            chunk_of,
            rows_out,
            exposures,
            halo,
            slot_ids,
            kernel_choice.T,
            bad_bands.T,
            row_range.T,
            flux_scale,
            vert_taps,
            horiz_taps,
        )
        return lists, count

    if rows_out == TILE_ROWS and expo_size == 2 * SQUARE:
        lists, count = block(lambda place, i: place ^ i ^ SQUARE)
        far, near = lists[:SQUARE], lists[SQUARE:]
        far = far[:1] + [swapped(part, "expo", 1 + i) for i, part in enumerate(far[1:])]
        near = near[:1] + [swapped(part, "expo", 1 + i) for i, part in enumerate(near[1:])]
        across = swapped(merge(far), "expo", SQUARE)
        coadd_plane, rejected_count = finish(near + [across], count, exposures_total)
    else:
        lists, count = block(lambda place, i: i)
        whole = jnp.concatenate(lists, 1)
        arrived = lax.all_to_all(whole, "expo", split_axis=1, concat_axis=0, tiled=True)
        arrived = arrived.reshape(expo_size, LISTS, rows_out, columns)
        coadd_plane, rejected_count = finish(
            [arrived[i] for i in range(expo_size)], count, exposures_total
        )
    return (coadd_plane[None], rejected_count[None])


def solution(mesh):
    in_specs = (
        P(("groups", "expo"), "sky", None),
        P("groups", None),
        P("groups", None),
        P("groups", None),
        P("groups", None),
        P("groups"),
        P("groups", None),
        P("groups", None),
    )
    out_specs = (P(("groups", "sky"), "expo", None), P(("groups", "sky"), "expo", None))
    return jax.shard_map(shards, mesh=mesh, in_specs=in_specs, out_specs=out_specs, check_vma=False)
```

```python
import functools

import jax
import jax.numpy as jnp
from jax import lax
from jax.experimental import pallas as pl
from jax.experimental.pallas import tpu as pltpu
from jax.sharding import PartitionSpec as P

BAND_COLS = 128
TAPS = 21
REJECT = 4
MIN_VALID = 12

SENTINEL = 1e30

TILE_ROWS = 16
PAD = 16
SQUARE = 4
KERNEL_VMEM = 8 * 1024 * 1024
LISTS = 2 * REJECT + 1


def sort_pair(entries, first, second, up):
    a, b = entries[first], entries[second]
    hi, lo = jnp.maximum(a, b), jnp.minimum(a, b)
    entries[first], entries[second] = (hi, lo) if up else (lo, hi)


def sorted_four(entries, up):
    entries = list(entries)
    for first, second in ((0, 1), (2, 3), (0, 2), (1, 3), (1, 2)):
        sort_pair(entries, first, second, up)
    return entries


def merged_four(left, right, up, ordered=True):
    pick = jnp.maximum if up else jnp.minimum
    entries = [pick(left[i], right[REJECT - 1 - i]) for i in range(REJECT)]
    if ordered:
        for first, second in ((0, 2), (1, 3), (0, 1), (2, 3)):
            sort_pair(entries, first, second, up)
    return entries


def valid_sum(highs, lows):
    total = None
    for value in highs + lows:
        wide = value.astype(jnp.float32)
        wide = jnp.where(jnp.abs(wide) < 0.5 * SENTINEL, wide, 0.0)
        total = wide if total is None else total + wide
    return total


def banded_pair(line):
    offset = lax.broadcasted_iota(jnp.int32, (BAND_COLS, BAND_COLS), 1) - (
        lax.broadcasted_iota(jnp.int32, (BAND_COLS, BAND_COLS), 0)
    )
    inside = jnp.abs(offset) < BAND_COLS // 2
    banded = pltpu.roll(
        jnp.broadcast_to(line, (BAND_COLS, BAND_COLS)), 0, 1, stride=1, stride_axis=0
    )
    return jnp.where(inside, banded, 0.0), jnp.where(inside, 0.0, banded)


def block_kernel(
    slots,
    bands,
    kernels,
    exposures_total,
    rows_out,
    chunk_of,
    exposures_ref,
    halo_ref,
    slot_hbm,
    choice_hbm,
    bad_hbm,
    range_hbm,
    flux_hbm,
    vert_hbm,
    horiz_hbm,
    *rest,
):
    rows = exposures_ref.shape[1]
    chunks = rows // TILE_ROWS
    outs, count_ref, rest = rest[:chunks], rest[chunks], rest[chunks + 1 :]
    (
        pictures,
        high,
        low,
        total,
        bank_v,
        bank_h,
        taps,
        bad_vec,
        range_vec,
        slot_ref,
        choice_ref,
        bad_ref,
        range_ref,
        flux_ref,
        sems,
        halo_sem,
        table_sems,
    ) = rest
    margin = TAPS // 2
    group = 4
    pieces = slots // group
    place = lax.axis_index("expo")
    sky_place = lax.axis_index("sky")

    tables = [
        pltpu.make_async_copy(source, target, table_sems.at[i])
        for i, (source, target) in enumerate(
            (
                (vert_hbm, taps.at[0]),
                (horiz_hbm, taps.at[1]),
                (slot_hbm, slot_ref),
                (choice_hbm, choice_ref),
                (bad_hbm, bad_ref),
                (range_hbm, range_ref),
                (flux_hbm, flux_ref),
                (bad_hbm, bad_vec),
                (range_hbm, range_vec),
            )
        )
    ]
    for copy in tables:
        copy.start()

    def body_copy(piece):
        return pltpu.make_async_copy(
            exposures_ref.at[pl.ds(piece * group, group)],
            pictures.at[pl.ds(piece * group, group), pl.ds(0, rows), :],
            sems.at[piece],
        )

    spot = pl.multiple_of(rows + PAD * (1 - sky_place), TILE_ROWS)
    bare = pl.multiple_of(rows + PAD * sky_place, TILE_ROWS)
    halo_copy = pltpu.make_async_copy(halo_ref, pictures.at[:, pl.ds(spot, PAD), :], halo_sem)
    halo_copy.start()
    for piece in range(pieces):
        body_copy(piece).start()
    pictures[:, pl.ds(bare, PAD), :] = jnp.zeros((slots, PAD, pictures.shape[2]), jnp.bfloat16)
    total[...] = jnp.zeros_like(total)

    tables[0].wait()
    tables[1].wait()
    wide = ((0, 0), (0, BAND_COLS - TAPS))
    vert_lines = jnp.pad(taps[0].astype(jnp.float32), wide)
    vert_lines = pltpu.roll(vert_lines, BAND_COLS - margin, 1)
    horiz_lines = jnp.pad(taps[1].astype(jnp.float32), wide)
    horiz_lines = pltpu.roll(horiz_lines, BAND_COLS - margin, 1)
    for kernel in range(kernels):
        main, edge = banded_pair(vert_lines[kernel : kernel + 1])
        bank_v[kernel, :, :BAND_COLS] = main.astype(jnp.bfloat16)
        bank_v[kernel, :, BAND_COLS:] = pltpu.roll(edge, PAD, 1)[:, : 2 * PAD].astype(jnp.bfloat16)
        main, edge = banded_pair(horiz_lines[kernel : kernel + 1])
        bank_h[kernel, :BAND_COLS] = main.T.astype(jnp.bfloat16)
        bank_h[kernel, BAND_COLS:] = edge.T.astype(jnp.bfloat16)
    for copy in tables[2:]:
        copy.wait()

    first_out = sky_place * rows + place * rows_out
    out_row = first_out + lax.broadcasted_iota(jnp.int32, (rows_out, exposures_total), 0)
    covered = (out_row >= range_vec[0:1, :]) & (out_row < range_vec[1:2, :])
    for band in range(bands):
        both = covered & (bad_vec[band : band + 1, :] == 0)
        number = jnp.sum(both.astype(jnp.float32), axis=1, keepdims=True)
        count_ref[:, band * BAND_COLS : (band + 1) * BAND_COLS] = jnp.broadcast_to(
            number.astype(jnp.int32), (rows_out, BAND_COLS)
        )

    row_index = sky_place * rows + lax.broadcasted_iota(jnp.int32, (rows, BAND_COLS), 0)
    lane = lax.broadcasted_iota(jnp.int32, (rows, BAND_COLS), 1)
    nothing = jnp.zeros((rows, BAND_COLS), jnp.bfloat16)

    def one_slot(slot):
        ident = slot_ref[place, slot]
        k = jnp.minimum(ident, exposures_total - 1)
        begin = range_ref[0, k]
        end = jnp.where(ident < exposures_total, range_ref[1, k], 0)
        factor = flux_ref[k]
        chosen = [choice_ref[band, k] for band in range(bands)]
        columns = []
        for band in range(bands):
            picture = pictures[slot, :, band * BAND_COLS : (band + 1) * BAND_COLS]
            vertical = jnp.dot(bank_v[chosen[band]], picture, preferred_element_type=jnp.float32)
            columns.append(vertical.astype(jnp.bfloat16))
        for band in range(bands):
            before = columns[band - 1] if band else nothing
            after = columns[band + 1] if band + 1 < bands else nothing
            sides = jnp.where(lane < BAND_COLS // 2, after, before)
            filtered = jnp.dot(
                jnp.concatenate([columns[band], sides], 1),
                bank_h[chosen[band]],
                preferred_element_type=jnp.float32,
            )
            plane = (filtered * factor).astype(jnp.bfloat16).astype(jnp.float32)
            stop = jnp.where(bad_ref[band, k] == 0, end, 0)
            usable = (row_index >= begin) & (row_index < stop)
            window = pl.ds(band * BAND_COLS, BAND_COLS)
            total[:, window] += jnp.where(usable, plane, 0.0)
            high[slot, :, window] = jnp.where(usable, plane, -SENTINEL).astype(jnp.bfloat16)
            low[slot, :, window] = jnp.where(usable, plane, SENTINEL).astype(jnp.bfloat16)

    halo_copy.wait()
    for piece in range(pieces):
        body_copy(piece).wait()

        def body(step, carry):
            one_slot(piece * group + 2 * step)
            one_slot(piece * group + 2 * step + 1)
            return carry

        lax.fori_loop(0, group // 2, body, 0)

    for position, out in enumerate(outs):
        top = pl.multiple_of(chunk_of(place, position) * TILE_ROWS, TILE_ROWS)

        def tiles(step, carry):
            for part in range(2):
                window = pl.ds(
                    pl.multiple_of((2 * step + part) * BAND_COLS, BAND_COLS), BAND_COLS
                )
                sides = []
                for source, up in ((high, True), (low, False)):
                    best = None
                    for piece in range(slots // REJECT):
                        entries = [
                            source[piece * REJECT + i, pl.ds(top, TILE_ROWS), window]
                            for i in range(REJECT)
                        ]
                        entries = sorted_four(entries, up)
                        best = entries if best is None else merged_four(best, entries, up)
                    sides.append(best)
                left = total[pl.ds(top, TILE_ROWS), window] - valid_sum(*sides)
                for index, value in enumerate(sides[0] + sides[1]):
                    out[index, :, window] = value
                out[2 * REJECT, :, window] = left.astype(jnp.bfloat16)
            return carry

        lax.fori_loop(0, bands // 2, tiles, 0)


def filter_block(chunk_of, rows_out, exposures, halo, slot_ids, choice, bad, span, flux, vert, horiz):
    slots, rows, columns = exposures.shape
    kernels = vert.shape[0]
    bands = columns // BAND_COLS
    chunks = rows // TILE_ROWS
    hbm = pl.BlockSpec(memory_space=pltpu.HBM)
    vmem = pl.BlockSpec(memory_space=pltpu.VMEM)
    anywhere = pl.BlockSpec(memory_space=pl.ANY)
    body = functools.partial(
        block_kernel, slots, bands, kernels, flux.shape[0], rows_out, chunk_of
    )
    return pl.pallas_call(
        body,
        out_shape=[jax.ShapeDtypeStruct((LISTS, TILE_ROWS, columns), jnp.bfloat16)] * chunks
        + [jax.ShapeDtypeStruct((rows_out, columns), jnp.int32)],
        in_specs=[hbm, anywhere] + [hbm] * 7,
        out_specs=[vmem] * (chunks + 1),
        scratch_shapes=[
            pltpu.VMEM((slots, rows + 2 * PAD, columns), jnp.bfloat16),
            pltpu.VMEM((slots, rows, columns), jnp.bfloat16),
            pltpu.VMEM((slots, rows, columns), jnp.bfloat16),
            pltpu.VMEM((rows, columns), jnp.float32),
            pltpu.VMEM((kernels, rows, BAND_COLS + 2 * PAD), jnp.bfloat16),
            pltpu.VMEM((kernels, 2 * BAND_COLS, BAND_COLS), jnp.bfloat16),
            pltpu.VMEM((2,) + vert.shape, jnp.bfloat16),
            pltpu.VMEM(bad.shape, jnp.int32),
            pltpu.VMEM(span.shape, jnp.int32),
            pltpu.SMEM(slot_ids.shape, jnp.int32),
            pltpu.SMEM(choice.shape, jnp.int32),
            pltpu.SMEM(bad.shape, jnp.int32),
            pltpu.SMEM(span.shape, jnp.int32),
            pltpu.SMEM(flux.shape, jnp.float32),
            pltpu.SemaphoreType.DMA((slots // 4,)),
            pltpu.SemaphoreType.DMA,
            pltpu.SemaphoreType.DMA((9,)),
        ],
        compiler_params=pltpu.CompilerParams(vmem_limit_bytes=40 * 1024 * 1024),
        cost_estimate=pl.CostEstimate(
            flops=4 * slots * rows * columns * 256, bytes_accessed=8 << 20, transcendentals=0
        ),
        name="filter_block",
    )(
        *[
            pltpu.with_memory_space_constraint(value, space)
            for value, space in zip(
                (exposures, halo, slot_ids, choice, bad, span, flux, vert, horiz),
                (pltpu.HBM, pltpu.VMEM) + (pltpu.HBM,) * 7,
                strict=True,
            )
        ]
    )


def merged_lists(refs, window, ordered):
    sides = []
    for base, up in ((0, True), (REJECT, False)):
        lists = [[ref[base + i, :, window] for i in range(REJECT)] for ref in refs]
        while len(lists) > 1:
            keep = ordered or len(lists) > 2
            paired = [
                merged_four(lists[i], lists[i + 1], up, keep)
                for i in range(0, len(lists) - 1, 2)
            ]
            lists = paired + (lists[-1:] if len(lists) % 2 else [])
        sides.append(lists[0])
    grand = None
    for ref in refs:
        part = ref[2 * REJECT, :, window].astype(jnp.float32) + valid_sum(
            [ref[i, :, window] for i in range(REJECT)],
            [ref[REJECT + i, :, window] for i in range(REJECT)],
        )
        grand = part if grand is None else grand + part
    return sides, grand


def merge_kernel(*refs):
    *sources, out = refs
    for band in range(out.shape[-1] // BAND_COLS):
        window = pl.ds(band * BAND_COLS, BAND_COLS)
        sides, grand = merged_lists(sources, window, True)
        for index, value in enumerate(sides[0] + sides[1]):
            out[index, :, window] = value
        out[2 * REJECT, :, window] = (grand - valid_sum(*sides)).astype(jnp.bfloat16)


def merge(parts):
    vmem = pl.BlockSpec(memory_space=pltpu.VMEM)
    return pl.pallas_call(
        merge_kernel,
        out_shape=jax.ShapeDtypeStruct(parts[0].shape, jnp.bfloat16),
        in_specs=[vmem] * len(parts),
        out_specs=vmem,
        compiler_params=pltpu.CompilerParams(vmem_limit_bytes=KERNEL_VMEM),
        name="merge_lists",
    )(*parts)


def finish_kernel(exposures_total, *refs):
    *sources, count_ref, coadd_ref, rejected_ref = refs
    for band in range(coadd_ref.shape[-1] // BAND_COLS):
        window = pl.ds(band * BAND_COLS, BAND_COLS)
        sides, grand = merged_lists(sources, window, False)
        extremes = valid_sum(*sides)
        count = count_ref[:, window]
        clipped = count >= MIN_VALID
        used = jnp.where(clipped, count - 2 * REJECT, count)
        kept = jnp.where(clipped, grand - extremes, grand)
        coadd_ref[:, window] = kept / jnp.maximum(used, 1).astype(jnp.float32)
        rejected_ref[:, window] = exposures_total - used


def finish(parts, count, exposures_total):
    vmem = pl.BlockSpec(memory_space=pltpu.VMEM)
    return pl.pallas_call(
        functools.partial(finish_kernel, exposures_total),
        out_shape=[
            jax.ShapeDtypeStruct(count.shape, jnp.float32),
            jax.ShapeDtypeStruct(count.shape, jnp.int32),
        ],
        in_specs=[vmem] * (len(parts) + 1),
        out_specs=[vmem, vmem],
        compiler_params=pltpu.CompilerParams(vmem_limit_bytes=KERNEL_VMEM),
        name="finish_pixels",
    )(*parts, count)


def swapped(value, axis, distance):
    count = lax.axis_size(axis)
    return lax.ppermute(value, axis, [(i, i ^ distance) for i in range(count)])


def shards(
    exposures, slot_ids, row_range, bad_bands, kernel_choice, flux_scale, vert_taps, horiz_taps
):
    slot_count, row_dev, columns = exposures.shape
    exposures_total = flux_scale.shape[0]
    expo_size = lax.axis_size("expo")
    sky_place = lax.axis_index("sky")
    rows_out = row_dev // expo_size

    edge_rows = lax.dynamic_slice_in_dim(exposures, (1 - sky_place) * (row_dev - PAD), PAD, 1)
    halo = swapped(edge_rows, "sky", 1)

    def block(chunk_of):
        *lists, count = filter_block(
            chunk_of,
            rows_out,
            exposures,
            halo,
            slot_ids,
            kernel_choice.T,
            bad_bands.T,
            row_range.T,
            flux_scale,
            vert_taps,
            horiz_taps,
        )
        return lists, count

    if rows_out == TILE_ROWS and expo_size == 2 * SQUARE:
        lists, count = block(lambda place, i: place ^ i ^ SQUARE)
        far, near = lists[:SQUARE], lists[SQUARE:]
        far = far[:1] + [swapped(part, "expo", 1 + i) for i, part in enumerate(far[1:])]
        near = near[:1] + [swapped(part, "expo", 1 + i) for i, part in enumerate(near[1:])]
        across = swapped(merge(far), "expo", SQUARE)
        coadd_plane, rejected_count = finish(near + [across], count, exposures_total)
    else:
        lists, count = block(lambda place, i: i)
        whole = jnp.concatenate(lists, 1)
        arrived = lax.all_to_all(whole, "expo", split_axis=1, concat_axis=0, tiled=True)
        arrived = arrived.reshape(expo_size, LISTS, rows_out, columns)
        coadd_plane, rejected_count = finish(
            [arrived[i] for i in range(expo_size)], count, exposures_total
        )
    return (coadd_plane[None], rejected_count[None])


def solution(mesh):
    in_specs = (
        P(("groups", "expo"), "sky", None),
        P("groups", None),
        P("groups", None),
        P("groups", None),
        P("groups", None),
        P("groups"),
        P("groups", None),
        P("groups", None),
    )
    out_specs = (P(("groups", "sky"), "expo", None), P(("groups", "sky"), "expo", None))
    return jax.shard_map(shards, mesh=mesh, in_specs=in_specs, out_specs=out_specs, check_vma=False)
```

```python
import functools

import jax
import jax.numpy as jnp
from jax import lax
from jax.experimental import pallas as pl
from jax.experimental.pallas import tpu as pltpu
from jax.sharding import PartitionSpec as P

BAND_COLS = 128
TAPS = 21
REJECT = 4
MIN_VALID = 12

SENTINEL = 1e30

TILE_ROWS = 16
PAD = 16
SQUARE = 4
KERNEL_VMEM = 8 * 1024 * 1024
LISTS = 2 * REJECT + 1


def sort_pair(entries, first, second, up):
    a, b = entries[first], entries[second]
    hi, lo = jnp.maximum(a, b), jnp.minimum(a, b)
    entries[first], entries[second] = (hi, lo) if up else (lo, hi)


def sorted_four(entries, up):
    entries = list(entries)
    for first, second in ((0, 1), (2, 3), (0, 2), (1, 3), (1, 2)):
        sort_pair(entries, first, second, up)
    return entries


def merged_four(left, right, up, ordered=True):
    pick = jnp.maximum if up else jnp.minimum
    entries = [pick(left[i], right[REJECT - 1 - i]) for i in range(REJECT)]
    if ordered:
        for first, second in ((0, 2), (1, 3), (0, 1), (2, 3)):
            sort_pair(entries, first, second, up)
    return entries


def extremes_sum(highs, lows):
    pairs = [h.astype(jnp.float32) + l.astype(jnp.float32) for h, l in zip(highs, lows, strict=True)]
    return functools.reduce(jnp.add, pairs)


def banded_pair(line):
    offset = lax.broadcasted_iota(jnp.int32, (BAND_COLS, BAND_COLS), 1) - (
        lax.broadcasted_iota(jnp.int32, (BAND_COLS, BAND_COLS), 0)
    )
    inside = jnp.abs(offset) < BAND_COLS // 2
    banded = pltpu.roll(
        jnp.broadcast_to(line, (BAND_COLS, BAND_COLS)), 0, 1, stride=1, stride_axis=0
    )
    return jnp.where(inside, banded, 0.0), jnp.where(inside, 0.0, banded)


def prepare_kernel(
    bands,
    kernels,
    rows_out,
    exposures_ref,
    slot_hbm,
    choice_hbm,
    bad_hbm,
    range_hbm,
    flux_hbm,
    vert_hbm,
    horiz_hbm,
    pictures,
    bank_v,
    bank_h,
    count_ref,
    slot_ref,
    choice_ref,
    bad_ref,
    range_ref,
    flux_ref,
    taps,
    sem,
    table_sems,
):
    rows = exposures_ref.shape[1]
    exposures_total = range_ref.shape[1]
    margin = TAPS // 2
    place = lax.axis_index("expo")
    sky_place = lax.axis_index("sky")
    tables = [
        pltpu.make_async_copy(source, target, table_sems.at[i])
        for i, (source, target) in enumerate(
            (
                (vert_hbm, taps.at[0]),
                (horiz_hbm, taps.at[1]),
                (slot_hbm, slot_ref),
                (choice_hbm, choice_ref),
                (bad_hbm, bad_ref),
                (range_hbm, range_ref),
                (flux_hbm, flux_ref),
            )
        )
    ]
    for copy in tables:
        copy.start()
    body_copy = pltpu.make_async_copy(exposures_ref, pictures, sem)
    body_copy.start()

    tables[0].wait()
    tables[1].wait()
    wide = ((0, 0), (0, BAND_COLS - TAPS))
    vert_lines = jnp.pad(taps[0].astype(jnp.float32), wide)
    vert_lines = pltpu.roll(vert_lines, BAND_COLS - margin, 1)
    horiz_lines = jnp.pad(taps[1].astype(jnp.float32), wide)
    horiz_lines = pltpu.roll(horiz_lines, BAND_COLS - margin, 1)
    turn = PAD * sky_place
    for kernel in range(kernels):
        main, edge = banded_pair(vert_lines[kernel : kernel + 1])
        bank_v[kernel, :, :BAND_COLS] = main.astype(jnp.bfloat16)
        bank_v[kernel, :, BAND_COLS:] = pltpu.roll(edge, turn, 1)[:, :PAD].astype(jnp.bfloat16)
        main, edge = banded_pair(horiz_lines[kernel : kernel + 1])
        edge = edge.T
        early = lax.broadcasted_iota(jnp.int32, edge.shape, 0) < BAND_COLS // 2
        before = jnp.where(early, 0.0, edge)
        after = jnp.where(early, edge, 0.0)
        for index, part in enumerate((before, main.T, after)):
            bank_h[kernel, index * BAND_COLS : (index + 1) * BAND_COLS] = part.astype(jnp.bfloat16)
    for copy in tables[2:]:
        copy.wait()

    first_out = sky_place * rows + place * rows_out
    out_row = first_out + lax.broadcasted_iota(jnp.int32, (rows_out, exposures_total), 0)
    covered = (out_row >= range_ref[0:1, :]) & (out_row < range_ref[1:2, :])
    for band in range(bands):
        both = covered & (bad_ref[band : band + 1, :] == 0)
        number = jnp.sum(both.astype(jnp.float32), axis=1, keepdims=True)
        count_ref[:, band * BAND_COLS : (band + 1) * BAND_COLS] = jnp.broadcast_to(
            number.astype(jnp.int32), (rows_out, BAND_COLS)
        )
    body_copy.wait()


def prepare(rows_out, exposures, slot_ids, choice, bad, span, flux, vert, horiz):
    rows, columns = exposures.shape[1:]
    kernels = vert.shape[0]
    bands = columns // BAND_COLS
    tables = [jax.ShapeDtypeStruct(t.shape, t.dtype) for t in (slot_ids, choice, bad, span, flux)]
    hbm = pl.BlockSpec(memory_space=pltpu.HBM)
    vmem = pl.BlockSpec(memory_space=pltpu.VMEM)
    return pl.pallas_call(
        functools.partial(prepare_kernel, bands, kernels, rows_out),
        out_shape=[
            jax.ShapeDtypeStruct(exposures.shape, jnp.bfloat16),
            jax.ShapeDtypeStruct((kernels, rows, BAND_COLS + PAD), jnp.bfloat16),
            jax.ShapeDtypeStruct((kernels, 3 * BAND_COLS, BAND_COLS), jnp.bfloat16),
            jax.ShapeDtypeStruct((rows_out, columns), jnp.int32),
        ]
        + tables,
        in_specs=[hbm] * 8,
        out_specs=[vmem] * 9,
        scratch_shapes=[
            pltpu.VMEM((2,) + vert.shape, jnp.bfloat16),
            pltpu.SemaphoreType.DMA,
            pltpu.SemaphoreType.DMA((7,)),
        ],
        compiler_params=pltpu.CompilerParams(vmem_limit_bytes=KERNEL_VMEM),
        cost_estimate=pl.CostEstimate(flops=1 << 20, bytes_accessed=4 << 20, transcendentals=0),
        name="prepare",
    )(
        *[
            pltpu.with_memory_space_constraint(value, pltpu.HBM)
            for value in (exposures, slot_ids, choice, bad, span, flux, vert, horiz)
        ]
    )


def select_chunk(top, high, low, total, out):
    slots, columns = high.shape[0], high.shape[2]

    def tiles(step, carry):
        for part in range(2):
            window = pl.ds(pl.multiple_of((2 * step + part) * BAND_COLS, BAND_COLS), BAND_COLS)
            sides = []
            for source, up in ((high, True), (low, False)):
                best = None
                for piece in range(slots // REJECT):
                    entries = [
                        source[piece * REJECT + i, pl.ds(top, TILE_ROWS), window]
                        for i in range(REJECT)
                    ]
                    entries = sorted_four(entries, up)
                    best = entries if best is None else merged_four(best, entries, up)
                sides.append(best)
            left = total[pl.ds(top, TILE_ROWS), window] - extremes_sum(*sides)
            for index, value in enumerate(sides[0] + sides[1]):
                out[index, :, window] = value
            out[2 * REJECT, :, window] = left.astype(jnp.bfloat16)
        return carry

    lax.fori_loop(0, columns // (2 * BAND_COLS), tiles, 0)


def filter_kernel(
    chunk_of,
    pictures,
    halo,
    bank_v,
    bank_h,
    slot_vmem,
    choice_vmem,
    bad_vmem,
    range_vmem,
    flux_vmem,
    high,
    low,
    total,
    *rest,
):
    *outs, slot_ref, choice_ref, bad_ref, range_ref, flux_ref, sems = rest
    slots, rows, columns = pictures.shape
    bands = columns // BAND_COLS
    exposures_total = range_vmem.shape[1]
    place = lax.axis_index("expo")
    sky_place = lax.axis_index("sky")
    tables = [
        pltpu.make_async_copy(source, target, sems.at[i])
        for i, (source, target) in enumerate(
            (
                (slot_vmem, slot_ref),
                (choice_vmem, choice_ref),
                (bad_vmem, bad_ref),
                (range_vmem, range_ref),
                (flux_vmem, flux_ref),
            )
        )
    ]
    for copy in tables:
        copy.start()
    total[...] = jnp.zeros_like(total)
    for copy in tables:
        copy.wait()

    row_index = sky_place * rows + lax.broadcasted_iota(jnp.int32, (rows, BAND_COLS), 0)
    lane = lax.broadcasted_iota(jnp.int32, (rows, BAND_COLS), 1)

    def one_slot(slot):
        ident = slot_ref[place, slot]
        k = jnp.minimum(ident, exposures_total - 1)
        begin = range_ref[0, k]
        end = jnp.where(ident < exposures_total, range_ref[1, k], 0)
        factor = flux_ref[k]
        chosen = [choice_ref[band, k] for band in range(bands)]
        verticals = []
        for band in range(bands):
            window = pl.ds(band * BAND_COLS, BAND_COLS)
            picture = jnp.concatenate([pictures[slot, :, window], halo[slot, :, window]], 0)
            vertical = jnp.dot(bank_v[chosen[band]], picture, preferred_element_type=jnp.float32)
            verticals.append(vertical.astype(jnp.bfloat16))
        filtered = []
        for band in range(0, bands, 2):
            pair = jnp.dot(
                jnp.concatenate(verticals[band : band + 2], 1),
                jnp.concatenate(
                    [bank_h[chosen[band], BAND_COLS:], bank_h[chosen[band + 1], : 2 * BAND_COLS]], 1
                ),
                preferred_element_type=jnp.float32,
            )
            filtered += [pair[:, :BAND_COLS], pair[:, BAND_COLS:]]
        for band in range(2, bands, 2):
            seam = jnp.dot(
                jnp.where(lane < BAND_COLS // 2, verticals[band], verticals[band - 1]),
                jnp.concatenate(
                    [
                        bank_h[chosen[band - 1], 2 * BAND_COLS :],
                        bank_h[chosen[band], :BAND_COLS],
                    ],
                    1,
                ),
                preferred_element_type=jnp.float32,
            )
            filtered[band - 1] += seam[:, :BAND_COLS]
            filtered[band] += seam[:, BAND_COLS:]
        for band in range(bands):
            plane = (filtered[band] * factor).astype(jnp.bfloat16).astype(jnp.float32)
            stop = jnp.where(bad_ref[band, k] == 0, end, 0)
            usable = (row_index >= begin) & (row_index < stop)
            window = pl.ds(band * BAND_COLS, BAND_COLS)
            total[:, window] += jnp.where(usable, plane, 0.0)
            high[slot, :, window] = jnp.where(usable, plane, -SENTINEL).astype(jnp.bfloat16)
            low[slot, :, window] = jnp.where(usable, plane, SENTINEL).astype(jnp.bfloat16)

    def body(step, carry):
        one_slot(2 * step)
        one_slot(2 * step + 1)
        return carry

    lax.fori_loop(0, slots // 2, body, 0)
    for position, out in enumerate(outs):
        top = pl.multiple_of(chunk_of(place, position) * TILE_ROWS, TILE_ROWS)
        select_chunk(top, high, low, total, out)


def filter_slots(chunk_of, chunks, pictures, halo, bank_v, bank_h, tables):
    slots, rows, columns = pictures.shape
    vmem = pl.BlockSpec(memory_space=pltpu.VMEM)
    return pl.pallas_call(
        functools.partial(filter_kernel, chunk_of),
        out_shape=[
            jax.ShapeDtypeStruct(pictures.shape, jnp.bfloat16),
            jax.ShapeDtypeStruct(pictures.shape, jnp.bfloat16),
            jax.ShapeDtypeStruct((rows, columns), jnp.float32),
        ]
        + [jax.ShapeDtypeStruct((LISTS, TILE_ROWS, columns), jnp.bfloat16)] * chunks,
        in_specs=[vmem] * (4 + len(tables)),
        out_specs=[vmem] * (3 + chunks),
        scratch_shapes=[pltpu.SMEM(table.shape, table.dtype) for table in tables]
        + [pltpu.SemaphoreType.DMA((len(tables),))],
        compiler_params=pltpu.CompilerParams(vmem_limit_bytes=KERNEL_VMEM),
        cost_estimate=pl.CostEstimate(
            flops=4 * slots * rows * columns * 256, bytes_accessed=8 << 20, transcendentals=0
        ),
        name="filter_slots",
    )(
        *[
            pltpu.with_memory_space_constraint(value, pltpu.VMEM)
            for value in (pictures, halo, bank_v, bank_h, *tables)
        ]
    )


def select_kernel(chunk_of, high, low, total, *outs):
    place = lax.axis_index("expo")
    for position, out in enumerate(outs):
        top = pl.multiple_of(chunk_of(place, position) * TILE_ROWS, TILE_ROWS)
        select_chunk(top, high, low, total, out)


def select(chunk_of, chunks, high, low, total):
    vmem = pl.BlockSpec(memory_space=pltpu.VMEM)
    return pl.pallas_call(
        functools.partial(select_kernel, chunk_of),
        out_shape=[jax.ShapeDtypeStruct((LISTS, TILE_ROWS, high.shape[2]), jnp.bfloat16)] * chunks,
        in_specs=[vmem] * 3,
        out_specs=[vmem] * chunks,
        compiler_params=pltpu.CompilerParams(vmem_limit_bytes=KERNEL_VMEM),
        cost_estimate=pl.CostEstimate(flops=1 << 24, bytes_accessed=4 << 20, transcendentals=0),
        name="select_rows",
    )(*[pltpu.with_memory_space_constraint(value, pltpu.VMEM) for value in (high, low, total)])


def merged_lists(refs, window, ordered):
    sides = []
    for base, up in ((0, True), (REJECT, False)):
        lists = [[ref[base + i, :, window] for i in range(REJECT)] for ref in refs]
        while len(lists) > 1:
            keep = ordered or len(lists) > 2
            paired = [
                merged_four(lists[i], lists[i + 1], up, keep)
                for i in range(0, len(lists) - 1, 2)
            ]
            lists = paired + (lists[-1:] if len(lists) % 2 else [])
        sides.append(lists[0])
    grand = None
    for ref in refs:
        part = ref[2 * REJECT, :, window].astype(jnp.float32) + extremes_sum(
            [ref[i, :, window] for i in range(REJECT)],
            [ref[REJECT + i, :, window] for i in range(REJECT)],
        )
        grand = part if grand is None else grand + part
    return sides, grand


def merge_kernel(*refs):
    *sources, out = refs
    for band in range(out.shape[-1] // BAND_COLS):
        window = pl.ds(band * BAND_COLS, BAND_COLS)
        sides, grand = merged_lists(sources, window, True)
        for index, value in enumerate(sides[0] + sides[1]):
            out[index, :, window] = value
        out[2 * REJECT, :, window] = (grand - extremes_sum(*sides)).astype(jnp.bfloat16)


def merge(parts):
    vmem = pl.BlockSpec(memory_space=pltpu.VMEM)
    return pl.pallas_call(
        merge_kernel,
        out_shape=jax.ShapeDtypeStruct(parts[0].shape, jnp.bfloat16),
        in_specs=[vmem] * len(parts),
        out_specs=vmem,
        compiler_params=pltpu.CompilerParams(vmem_limit_bytes=KERNEL_VMEM),
        name="merge_lists",
    )(*parts)


def finish_kernel(exposures_total, *refs):
    *sources, count_ref, coadd_ref, rejected_ref = refs
    for band in range(coadd_ref.shape[-1] // BAND_COLS):
        window = pl.ds(band * BAND_COLS, BAND_COLS)
        sides, grand = merged_lists(sources, window, False)
        extremes = extremes_sum(*sides)
        count = count_ref[:, window]
        clipped = count >= MIN_VALID
        used = jnp.where(clipped, count - 2 * REJECT, count)
        kept = jnp.where(clipped, grand - extremes, grand)
        coadd_ref[:, window] = kept / jnp.maximum(used, 1).astype(jnp.float32)
        rejected_ref[:, window] = exposures_total - used


def finish(parts, count, exposures_total):
    vmem = pl.BlockSpec(memory_space=pltpu.VMEM)
    return pl.pallas_call(
        functools.partial(finish_kernel, exposures_total),
        out_shape=[
            jax.ShapeDtypeStruct(count.shape, jnp.float32),
            jax.ShapeDtypeStruct(count.shape, jnp.int32),
        ],
        in_specs=[vmem] * (len(parts) + 1),
        out_specs=[vmem, vmem],
        compiler_params=pltpu.CompilerParams(vmem_limit_bytes=KERNEL_VMEM),
        name="finish_pixels",
    )(*parts, count)


def swapped(value, axis, distance):
    count = lax.axis_size(axis)
    return lax.ppermute(value, axis, [(i, i ^ distance) for i in range(count)])


def shards(
    exposures, slot_ids, row_range, bad_bands, kernel_choice, flux_scale, vert_taps, horiz_taps
):
    slot_count, row_dev, columns = exposures.shape
    exposures_total = flux_scale.shape[0]
    expo_size = lax.axis_size("expo")
    sky_place = lax.axis_index("sky")
    rows_out = row_dev // expo_size

    edge_rows = lax.dynamic_slice_in_dim(exposures, (1 - sky_place) * (row_dev - PAD), PAD, 1)
    halo = swapped(edge_rows, "sky", 1)

    pictures, bank_v, bank_h, count, *tables = prepare(
        rows_out,
        exposures,
        slot_ids,
        kernel_choice.T,
        bad_bands.T,
        row_range.T,
        flux_scale,
        vert_taps,
        horiz_taps,
    )

    if rows_out == TILE_ROWS and expo_size == 2 * SQUARE:
        high, low, total, *far = filter_slots(
            lambda place, i: place ^ i ^ SQUARE, SQUARE, pictures, halo, bank_v, bank_h, tables
        )
        far = far[:1] + [swapped(part, "expo", 1 + i) for i, part in enumerate(far[1:])]
        near = list(select(lambda place, i: place ^ i, SQUARE, high, low, total))
        near = near[:1] + [swapped(part, "expo", 1 + i) for i, part in enumerate(near[1:])]
        across = swapped(merge(far), "expo", SQUARE)
        coadd_plane, rejected_count = finish(near + [across], count, exposures_total)
    else:
        chunks = row_dev // TILE_ROWS
        high, low, total, *lists = filter_slots(
            lambda place, i: i, chunks, pictures, halo, bank_v, bank_h, tables
        )
        whole = jnp.concatenate(lists, 1)
        arrived = lax.all_to_all(whole, "expo", split_axis=1, concat_axis=0, tiled=True)
        arrived = arrived.reshape(expo_size, LISTS, rows_out, columns)
        coadd_plane, rejected_count = finish(
            [arrived[i] for i in range(expo_size)], count, exposures_total
        )
    return (coadd_plane[None], rejected_count[None])


def solution(mesh):
    in_specs = (
        P(("groups", "expo"), "sky", None),
        P("groups", None),
        P("groups", None),
        P("groups", None),
        P("groups", None),
        P("groups"),
        P("groups", None),
        P("groups", None),
    )
    out_specs = (P(("groups", "sky"), "expo", None), P(("groups", "sky"), "expo", None))
    return jax.shard_map(shards, mesh=mesh, in_specs=in_specs, out_specs=out_specs, check_vma=False)
```

```python
import functools

import jax
import jax.numpy as jnp
from jax import lax
from jax.experimental import pallas as pl
from jax.experimental.pallas import tpu as pltpu
from jax.sharding import PartitionSpec as P

BAND_COLS = 128
TAPS = 21
REJECT = 4
MIN_VALID = 12

SENTINEL = 1e30

TILE_ROWS = 16
PAD = 16
STRIDE = 8
FAR_PARTS = 2
SQUARE = 4
KERNEL_VMEM = 8 * 1024 * 1024
LISTS = 2 * REJECT + 1


def sort_pair(entries, first, second, up):
    a, b = entries[first], entries[second]
    hi, lo = jnp.maximum(a, b), jnp.minimum(a, b)
    entries[first], entries[second] = (hi, lo) if up else (lo, hi)


def sorted_four(entries, up):
    entries = list(entries)
    for first, second in ((0, 1), (2, 3), (0, 2), (1, 3), (1, 2)):
        sort_pair(entries, first, second, up)
    return entries


def merged_four(left, right, up, ordered=True):
    pick = jnp.maximum if up else jnp.minimum
    entries = [pick(left[i], right[REJECT - 1 - i]) for i in range(REJECT)]
    if ordered:
        for first, second in ((0, 2), (1, 3), (0, 1), (2, 3)):
            sort_pair(entries, first, second, up)
    return entries


def extremes_sum(highs, lows):
    pairs = [h.astype(jnp.float32) + l.astype(jnp.float32) for h, l in zip(highs, lows, strict=True)]
    return functools.reduce(jnp.add, pairs)


def banded_pair(line):
    offset = lax.broadcasted_iota(jnp.int32, (BAND_COLS, BAND_COLS), 1) - (
        lax.broadcasted_iota(jnp.int32, (BAND_COLS, BAND_COLS), 0)
    )
    inside = jnp.abs(offset) < BAND_COLS // 2
    banded = pltpu.roll(
        jnp.broadcast_to(line, (BAND_COLS, BAND_COLS)), 0, 1, stride=1, stride_axis=0
    )
    return jnp.where(inside, banded, 0.0), jnp.where(inside, 0.0, banded)


def prepare_kernel(
    bands,
    kernels,
    rows_out,
    exposures_ref,
    slot_hbm,
    choice_hbm,
    bad_hbm,
    range_hbm,
    flux_hbm,
    vert_hbm,
    horiz_hbm,
    pictures,
    bank_v,
    bank_h,
    count_ref,
    slot_ref,
    choice_ref,
    bad_ref,
    range_ref,
    flux_ref,
    taps,
    sem,
    table_sems,
):
    rows = exposures_ref.shape[1]
    exposures_total = range_ref.shape[1]
    margin = TAPS // 2
    place = lax.axis_index("expo")
    sky_place = lax.axis_index("sky")
    tables = [
        pltpu.make_async_copy(source, target, table_sems.at[i])
        for i, (source, target) in enumerate(
            (
                (vert_hbm, taps.at[0]),
                (horiz_hbm, taps.at[1]),
                (slot_hbm, slot_ref),
                (choice_hbm, choice_ref),
                (bad_hbm, bad_ref),
                (range_hbm, range_ref),
                (flux_hbm, flux_ref),
            )
        )
    ]
    for copy in tables:
        copy.start()
    body_copy = pltpu.make_async_copy(exposures_ref, pictures, sem)
    body_copy.start()

    tables[0].wait()
    tables[1].wait()
    wide = ((0, 0), (0, BAND_COLS - TAPS))
    vert_lines = jnp.pad(taps[0].astype(jnp.float32), wide)
    vert_lines = pltpu.roll(vert_lines, BAND_COLS - margin, 1)
    horiz_lines = jnp.pad(taps[1].astype(jnp.float32), wide)
    horiz_lines = pltpu.roll(horiz_lines, BAND_COLS - margin, 1)
    turn = PAD * sky_place
    for kernel in range(kernels):
        main, edge = banded_pair(vert_lines[kernel : kernel + 1])
        bank_v[kernel, :, :BAND_COLS] = main.astype(jnp.bfloat16)
        bank_v[kernel, :, BAND_COLS:] = pltpu.roll(edge, turn, 1)[:, :PAD].astype(jnp.bfloat16)
        main, edge = banded_pair(horiz_lines[kernel : kernel + 1])
        edge = edge.T
        early = lax.broadcasted_iota(jnp.int32, edge.shape, 0) < BAND_COLS // 2
        before = jnp.where(early, 0.0, edge)
        after = jnp.where(early, edge, 0.0)
        for index, part in enumerate((before, main.T, after)):
            bank_h[kernel, index * BAND_COLS : (index + 1) * BAND_COLS] = part.astype(jnp.bfloat16)
    for copy in tables[2:]:
        copy.wait()

    first_out = sky_place * rows + place * rows_out
    out_row = first_out + lax.broadcasted_iota(jnp.int32, (rows_out, exposures_total), 0)
    covered = (out_row >= range_ref[0:1, :]) & (out_row < range_ref[1:2, :])
    for band in range(bands):
        both = covered & (bad_ref[band : band + 1, :] == 0)
        number = jnp.sum(both.astype(jnp.float32), axis=1, keepdims=True)
        count_ref[:, band * BAND_COLS : (band + 1) * BAND_COLS] = jnp.broadcast_to(
            number.astype(jnp.int32), (rows_out, BAND_COLS)
        )
    body_copy.wait()


def prepare(rows_out, exposures, slot_ids, choice, bad, span, flux, vert, horiz):
    rows, columns = exposures.shape[1:]
    kernels = vert.shape[0]
    bands = columns // BAND_COLS
    tables = [jax.ShapeDtypeStruct(t.shape, t.dtype) for t in (slot_ids, choice, bad, span, flux)]
    hbm = pl.BlockSpec(memory_space=pltpu.HBM)
    vmem = pl.BlockSpec(memory_space=pltpu.VMEM)
    return pl.pallas_call(
        functools.partial(prepare_kernel, bands, kernels, rows_out),
        out_shape=[
            jax.ShapeDtypeStruct(exposures.shape, jnp.bfloat16),
            jax.ShapeDtypeStruct((kernels, rows, BAND_COLS + PAD), jnp.bfloat16),
            jax.ShapeDtypeStruct((kernels, 3 * BAND_COLS, BAND_COLS), jnp.bfloat16),
            jax.ShapeDtypeStruct((rows_out, columns), jnp.int32),
        ]
        + tables,
        in_specs=[hbm] * 8,
        out_specs=[vmem] * 9,
        scratch_shapes=[
            pltpu.VMEM((2,) + vert.shape, jnp.bfloat16),
            pltpu.SemaphoreType.DMA,
            pltpu.SemaphoreType.DMA((7,)),
        ],
        compiler_params=pltpu.CompilerParams(vmem_limit_bytes=KERNEL_VMEM),
        cost_estimate=pl.CostEstimate(flops=1 << 20, bytes_accessed=4 << 20, transcendentals=0),
        name="prepare",
    )(
        *[
            pltpu.with_memory_space_constraint(value, pltpu.HBM)
            for value in (exposures, slot_ids, choice, bad, span, flux, vert, horiz)
        ]
    )


def select_chunk(top, high, low, total, outs):
    slots, _, columns = high.shape
    windows = [pl.ds(start, BAND_COLS) for start in range(0, columns, BAND_COLS)]
    streams = [(w, source, up) for w in windows for source, up in ((high, True), (low, False))]
    best = [None] * len(streams)
    for piece in range(slots // REJECT):
        for n, (window, source, up) in enumerate(streams):
            entries = [
                source[piece * REJECT + i, pl.ds(top, TILE_ROWS), window] for i in range(REJECT)
            ]
            entries = sorted_four(entries, up)
            best[n] = entries if best[n] is None else merged_four(best[n], entries, up)
    bands_each = len(windows) // len(outs)
    for n, window in enumerate(windows):
        sides = best[2 * n : 2 * n + 2]
        left = total[pl.ds(top, TILE_ROWS), window] - extremes_sum(*sides)
        out = outs[n // bands_each]
        place = pl.ds((n % bands_each) * BAND_COLS, BAND_COLS)
        for index, value in enumerate(sides[0] + sides[1]):
            out[index, :, place] = value
        out[2 * REJECT, :, place] = left.astype(jnp.bfloat16)


def select_chunks(chunk_of, parts, high, low, total, outs):
    place = lax.axis_index("expo")
    for position in range(len(outs) // parts):
        top = pl.multiple_of(chunk_of(place, position) * TILE_ROWS, TILE_ROWS)
        select_chunk(top, high, low, total, outs[position * parts : (position + 1) * parts])


def filter_kernel(
    chunk_of,
    parts,
    pictures,
    halo,
    bank_v,
    bank_h,
    slot_vmem,
    choice_vmem,
    bad_vmem,
    range_vmem,
    flux_vmem,
    high,
    low,
    total,
    *rest,
):
    *outs, slot_ref, choice_ref, bad_ref, range_ref, flux_ref, sems = rest
    slots, rows, columns = pictures.shape
    bands = columns // BAND_COLS
    exposures_total = range_vmem.shape[1]
    place = lax.axis_index("expo")
    sky_place = lax.axis_index("sky")
    tables = [
        pltpu.make_async_copy(source, target, sems.at[i])
        for i, (source, target) in enumerate(
            (
                (slot_vmem, slot_ref),
                (choice_vmem, choice_ref),
                (bad_vmem, bad_ref),
                (range_vmem, range_ref),
                (flux_vmem, flux_ref),
            )
        )
    ]
    for copy in tables:
        copy.start()
    total[...] = jnp.zeros_like(total)
    for copy in tables:
        copy.wait()

    row_index = lax.broadcasted_iota(jnp.int32, (rows, BAND_COLS), 0)
    row_index = (row_index + sky_place * rows).astype(jnp.float32).astype(jnp.bfloat16)
    zero = jnp.zeros((), jnp.bfloat16)
    sentinel = jnp.asarray(SENTINEL, jnp.bfloat16)
    lane = lax.broadcasted_iota(jnp.int32, (rows, BAND_COLS), 1)

    def first_pass(slot):
        ident = slot_ref[place, slot]
        k = jnp.minimum(ident, exposures_total - 1)
        begin = range_ref[0, k]
        end = jnp.where(ident < exposures_total, range_ref[1, k], 0)
        factor = flux_ref[k]
        chosen = [choice_ref[band, k] for band in range(bands)]
        verticals = []
        for band in range(bands):
            window = pl.ds(band * BAND_COLS, BAND_COLS)
            picture = jnp.concatenate([pictures[slot, :, window], halo[slot, :, window]], 0)
            vertical = jnp.dot(bank_v[chosen[band]], picture, preferred_element_type=jnp.float32)
            verticals.append(vertical.astype(jnp.bfloat16))
        return k, factor, chosen, begin, end, verticals

    def second_pass(slot, k, factor, chosen, begin, end, verticals):
        filtered = []
        for band in range(0, bands, 2):
            pair = jnp.dot(
                jnp.concatenate(verticals[band : band + 2], 1),
                jnp.concatenate(
                    [bank_h[chosen[band], BAND_COLS:], bank_h[chosen[band + 1], : 2 * BAND_COLS]], 1
                ),
                preferred_element_type=jnp.float32,
            )
            filtered += [pair[:, :BAND_COLS], pair[:, BAND_COLS:]]
        for band in range(2, bands, 2):
            seam = jnp.dot(
                jnp.where(lane < BAND_COLS // 2, verticals[band], verticals[band - 1]),
                jnp.concatenate(
                    [
                        bank_h[chosen[band - 1], 2 * BAND_COLS :],
                        bank_h[chosen[band], :BAND_COLS],
                    ],
                    1,
                ),
                preferred_element_type=jnp.float32,
            )
            filtered[band - 1] += seam[:, :BAND_COLS]
            filtered[band] += seam[:, BAND_COLS:]
        first_row = begin.astype(jnp.float32).astype(jnp.bfloat16)
        for band in range(bands):
            plane = (filtered[band] * factor).astype(jnp.bfloat16)
            stop = jnp.where(bad_ref[band, k] == 0, end, 0).astype(jnp.float32)
            usable = (row_index >= first_row) & (row_index < stop.astype(jnp.bfloat16))
            window = pl.ds(band * BAND_COLS, BAND_COLS)
            total[:, window] += jnp.where(usable, plane, zero).astype(jnp.float32)
            high[slot, :, window] = jnp.where(usable, plane, -sentinel)
            low[slot, :, window] = jnp.where(usable, plane, sentinel)

    def body(step, carry):
        held = first_pass(STRIDE * step)
        for i in range(STRIDE):
            ahead = first_pass(STRIDE * step + i + 1) if i + 1 < STRIDE else None
            second_pass(STRIDE * step + i, *held)
            held = ahead
        return carry

    lax.fori_loop(0, slots // STRIDE, body, 0)
    select_chunks(chunk_of, parts, high, low, total, outs)


def filter_slots(chunk_of, chunks, parts, pictures, halo, bank_v, bank_h, tables):
    slots, rows, columns = pictures.shape
    vmem = pl.BlockSpec(memory_space=pltpu.VMEM)
    return pl.pallas_call(
        functools.partial(filter_kernel, chunk_of, parts),
        out_shape=[
            jax.ShapeDtypeStruct(pictures.shape, jnp.bfloat16),
            jax.ShapeDtypeStruct(pictures.shape, jnp.bfloat16),
            jax.ShapeDtypeStruct((rows, columns), jnp.float32),
        ]
        + [jax.ShapeDtypeStruct((LISTS, TILE_ROWS, columns // parts), jnp.bfloat16)]
        * (chunks * parts),
        in_specs=[vmem] * (4 + len(tables)),
        out_specs=[vmem] * (3 + chunks * parts),
        scratch_shapes=[pltpu.SMEM(table.shape, table.dtype) for table in tables]
        + [pltpu.SemaphoreType.DMA((len(tables),))],
        compiler_params=pltpu.CompilerParams(vmem_limit_bytes=KERNEL_VMEM),
        cost_estimate=pl.CostEstimate(
            flops=4 * slots * rows * columns * 256, bytes_accessed=8 << 20, transcendentals=0
        ),
        name="filter_slots",
    )(
        *[
            pltpu.with_memory_space_constraint(value, pltpu.VMEM)
            for value in (pictures, halo, bank_v, bank_h, *tables)
        ]
    )


def select_kernel(chunk_of, parts, high, low, total, *outs):
    select_chunks(chunk_of, parts, high, low, total, outs)


def select(chunk_of, chunks, parts, high, low, total):
    vmem = pl.BlockSpec(memory_space=pltpu.VMEM)
    return pl.pallas_call(
        functools.partial(select_kernel, chunk_of, parts),
        out_shape=[
            jax.ShapeDtypeStruct((LISTS, TILE_ROWS, high.shape[2] // parts), jnp.bfloat16)
        ]
        * (chunks * parts),
        in_specs=[vmem] * 3,
        out_specs=[vmem] * (chunks * parts),
        compiler_params=pltpu.CompilerParams(vmem_limit_bytes=KERNEL_VMEM),
        cost_estimate=pl.CostEstimate(flops=1 << 24, bytes_accessed=4 << 20, transcendentals=0),
        name="select_rows",
    )(*[pltpu.with_memory_space_constraint(value, pltpu.VMEM) for value in (high, low, total)])


def merged_lists(sources, ordered):
    sides = []
    for base, up in ((0, True), (REJECT, False)):
        lists = [[ref[base + i, :, window] for i in range(REJECT)] for ref, window in sources]
        while len(lists) > 1:
            keep = ordered or len(lists) > 2
            paired = [
                merged_four(lists[i], lists[i + 1], up, keep)
                for i in range(0, len(lists) - 1, 2)
            ]
            lists = paired + (lists[-1:] if len(lists) % 2 else [])
        sides.append(lists[0])
    grand = None
    for ref, window in sources:
        part = ref[2 * REJECT, :, window].astype(jnp.float32) + extremes_sum(
            [ref[i, :, window] for i in range(REJECT)],
            [ref[REJECT + i, :, window] for i in range(REJECT)],
        )
        grand = part if grand is None else grand + part
    return sides, grand


def merge_kernel(*refs):
    *sources, out = refs
    for band in range(out.shape[-1] // BAND_COLS):
        window = pl.ds(band * BAND_COLS, BAND_COLS)
        sides, grand = merged_lists([(ref, window) for ref in sources], True)
        for index, value in enumerate(sides[0] + sides[1]):
            out[index, :, window] = value
        out[2 * REJECT, :, window] = (grand - extremes_sum(*sides)).astype(jnp.bfloat16)


def merge(parts):
    vmem = pl.BlockSpec(memory_space=pltpu.VMEM)
    return pl.pallas_call(
        merge_kernel,
        out_shape=jax.ShapeDtypeStruct(parts[0].shape, jnp.bfloat16),
        in_specs=[vmem] * len(parts),
        out_specs=vmem,
        compiler_params=pltpu.CompilerParams(vmem_limit_bytes=KERNEL_VMEM),
        name="merge_lists",
    )(*parts)


def finish_kernel(exposures_total, whole, *refs):
    *sources, count_ref, coadd_ref, rejected_ref = refs
    whole, parts = sources[:whole], sources[whole:]
    for band in range(coadd_ref.shape[-1] // BAND_COLS):
        window = pl.ds(band * BAND_COLS, BAND_COLS)
        here = [(ref, window) for ref in whole]
        for index, ref in enumerate(parts):
            first, held = index * ref.shape[-1], ref.shape[-1]
            if first <= band * BAND_COLS < first + held:
                here.append((ref, pl.ds(band * BAND_COLS - first, BAND_COLS)))
        sides, grand = merged_lists(here, False)
        extremes = extremes_sum(*sides)
        count = count_ref[:, window]
        clipped = count >= MIN_VALID
        used = jnp.where(clipped, count - 2 * REJECT, count)
        kept = jnp.where(clipped, grand - extremes, grand)
        coadd_ref[:, window] = kept / jnp.maximum(used, 1).astype(jnp.float32)
        rejected_ref[:, window] = exposures_total - used


def finish(whole, parts, count, exposures_total):
    vmem = pl.BlockSpec(memory_space=pltpu.VMEM)
    return pl.pallas_call(
        functools.partial(finish_kernel, exposures_total, len(whole)),
        out_shape=[
            jax.ShapeDtypeStruct(count.shape, jnp.float32),
            jax.ShapeDtypeStruct(count.shape, jnp.int32),
        ],
        in_specs=[vmem] * (len(whole) + len(parts) + 1),
        out_specs=[vmem, vmem],
        compiler_params=pltpu.CompilerParams(vmem_limit_bytes=KERNEL_VMEM),
        name="finish_pixels",
    )(*whole, *parts, count)


def swapped(value, axis, distance):
    count = lax.axis_size(axis)
    return lax.ppermute(value, axis, [(i, i ^ distance) for i in range(count)])


def shards(
    exposures, slot_ids, row_range, bad_bands, kernel_choice, flux_scale, vert_taps, horiz_taps
):
    slot_count, row_dev, columns = exposures.shape
    exposures_total = flux_scale.shape[0]
    expo_size = lax.axis_size("expo")
    sky_place = lax.axis_index("sky")
    rows_out = row_dev // expo_size

    edge_rows = lax.dynamic_slice_in_dim(exposures, (1 - sky_place) * (row_dev - PAD), PAD, 1)
    halo = swapped(edge_rows, "sky", 1)

    pictures, bank_v, bank_h, count, *tables = prepare(
        rows_out,
        exposures,
        slot_ids,
        kernel_choice.T,
        bad_bands.T,
        row_range.T,
        flux_scale,
        vert_taps,
        horiz_taps,
    )

    if rows_out == TILE_ROWS and expo_size == 2 * SQUARE:
        high, low, total, *far = filter_slots(
            lambda place, i: place ^ i ^ SQUARE,
            SQUARE,
            FAR_PARTS,
            pictures,
            halo,
            bank_v,
            bank_h,
            tables,
        )
        across = []
        for part in range(FAR_PARTS):
            own, *sent = far[part::FAR_PARTS]
            got = [swapped(sent[i], "expo", 1 + i) for i in reversed(range(SQUARE - 1))]
            across.append(swapped(merge([own] + got), "expo", SQUARE))
        near = list(select(lambda place, i: place ^ i, SQUARE, 1, high, low, total))
        near = near[:1] + [swapped(part, "expo", 1 + i) for i, part in enumerate(near[1:])]
        coadd_plane, rejected_count = finish(near, across, count, exposures_total)
    else:
        chunks = row_dev // TILE_ROWS
        high, low, total, *lists = filter_slots(
            lambda place, i: i, chunks, 1, pictures, halo, bank_v, bank_h, tables
        )
        whole = jnp.concatenate(lists, 1)
        arrived = lax.all_to_all(whole, "expo", split_axis=1, concat_axis=0, tiled=True)
        arrived = arrived.reshape(expo_size, LISTS, rows_out, columns)
        coadd_plane, rejected_count = finish(
            [arrived[i] for i in range(expo_size)], [], count, exposures_total
        )
    return (coadd_plane[None], rejected_count[None])


def solution(mesh):
    in_specs = (
        P(("groups", "expo"), "sky", None),
        P("groups", None),
        P("groups", None),
        P("groups", None),
        P("groups", None),
        P("groups"),
        P("groups", None),
        P("groups", None),
    )
    out_specs = (P(("groups", "sky"), "expo", None), P(("groups", "sky"), "expo", None))
    return jax.shard_map(shards, mesh=mesh, in_specs=in_specs, out_specs=out_specs, check_vma=False)
```

```python
import functools

import jax
import jax.numpy as jnp
from jax import lax
from jax.experimental import pallas as pl
from jax.experimental.pallas import tpu as pltpu
from jax.sharding import PartitionSpec as P

BAND_COLS = 128
TAPS = 21
REJECT = 4
MIN_VALID = 12

SENTINEL = 1e30

TILE_ROWS = 16
PAD = 16
STRIDE = 8
FAR_PARTS = 1
SQUARE = 4
KERNEL_VMEM = 8 * 1024 * 1024
LISTS = 2 * REJECT + 1


def sort_pair(entries, first, second, up):
    a, b = entries[first], entries[second]
    hi, lo = jnp.maximum(a, b), jnp.minimum(a, b)
    entries[first], entries[second] = (hi, lo) if up else (lo, hi)


def sorted_four(entries, up):
    entries = list(entries)
    for first, second in ((0, 1), (2, 3), (0, 2), (1, 3), (1, 2)):
        sort_pair(entries, first, second, up)
    return entries


def merged_four(left, right, up, ordered=True):
    pick = jnp.maximum if up else jnp.minimum
    entries = [pick(left[i], right[REJECT - 1 - i]) for i in range(REJECT)]
    if ordered:
        for first, second in ((0, 2), (1, 3), (0, 1), (2, 3)):
            sort_pair(entries, first, second, up)
    return entries


def extremes_sum(highs, lows):
    pairs = [h.astype(jnp.float32) + l.astype(jnp.float32) for h, l in zip(highs, lows, strict=True)]
    return functools.reduce(jnp.add, pairs)


def banded_pair(line):
    offset = lax.broadcasted_iota(jnp.int32, (BAND_COLS, BAND_COLS), 1) - (
        lax.broadcasted_iota(jnp.int32, (BAND_COLS, BAND_COLS), 0)
    )
    inside = jnp.abs(offset) < BAND_COLS // 2
    banded = pltpu.roll(
        jnp.broadcast_to(line, (BAND_COLS, BAND_COLS)), 0, 1, stride=1, stride_axis=0
    )
    return jnp.where(inside, banded, 0.0), jnp.where(inside, 0.0, banded)


def bank_lines(taps, margin):
    lines = jnp.pad(taps.astype(jnp.float32), ((0, 0), (0, BAND_COLS - TAPS)))
    return pltpu.roll(lines, BAND_COLS - margin, 1)


def edge_kernel(exposures_ref, vert_hbm, edge_ref, bank_v, taps, sems):
    rows = exposures_ref.shape[1]
    sky_place = lax.axis_index("sky")
    start = pl.multiple_of((1 - sky_place) * (rows - PAD), TILE_ROWS)
    edge_copy = pltpu.make_async_copy(
        exposures_ref.at[:, pl.ds(start, PAD), :], edge_ref, sems.at[0]
    )
    taps_copy = pltpu.make_async_copy(vert_hbm, taps, sems.at[1])
    taps_copy.start()
    edge_copy.start()
    taps_copy.wait()
    lines = bank_lines(taps[...], TAPS // 2)
    turn = PAD * sky_place
    for kernel in range(taps.shape[0]):
        main, edge = banded_pair(lines[kernel : kernel + 1])
        bank_v[kernel, :, :BAND_COLS] = main.astype(jnp.bfloat16)
        bank_v[kernel, :, BAND_COLS:] = pltpu.roll(edge, turn, 1)[:, :PAD].astype(jnp.bfloat16)
    edge_copy.wait()


def window_edges(exposures, vert):
    slots, rows, columns = exposures.shape
    hbm = pl.BlockSpec(memory_space=pltpu.HBM)
    vmem = pl.BlockSpec(memory_space=pltpu.VMEM)
    return pl.pallas_call(
        edge_kernel,
        out_shape=[
            jax.ShapeDtypeStruct((slots, PAD, columns), jnp.bfloat16),
            jax.ShapeDtypeStruct((vert.shape[0], rows, BAND_COLS + PAD), jnp.bfloat16),
        ],
        in_specs=[hbm] * 2,
        out_specs=[vmem] * 2,
        scratch_shapes=[pltpu.VMEM(vert.shape, jnp.bfloat16), pltpu.SemaphoreType.DMA((2,))],
        compiler_params=pltpu.CompilerParams(vmem_limit_bytes=KERNEL_VMEM),
        name="window_edges",
    )(*[pltpu.with_memory_space_constraint(value, pltpu.HBM) for value in (exposures, vert)])


def prepare_kernel(
    bands,
    rows_out,
    exposures_ref,
    slot_hbm,
    choice_hbm,
    bad_hbm,
    range_hbm,
    flux_hbm,
    horiz_hbm,
    pictures,
    bank_h,
    count_ref,
    slot_ref,
    choice_ref,
    bad_ref,
    range_ref,
    flux_ref,
    taps,
    sem,
    table_sems,
):
    rows = exposures_ref.shape[1]
    exposures_total = range_ref.shape[1]
    place = lax.axis_index("expo")
    sky_place = lax.axis_index("sky")
    tables = [
        pltpu.make_async_copy(source, target, table_sems.at[i])
        for i, (source, target) in enumerate(
            (
                (horiz_hbm, taps),
                (slot_hbm, slot_ref),
                (choice_hbm, choice_ref),
                (bad_hbm, bad_ref),
                (range_hbm, range_ref),
                (flux_hbm, flux_ref),
            )
        )
    ]
    for copy in tables:
        copy.start()
    body_copy = pltpu.make_async_copy(
        exposures_ref.at[pl.ds(0, STRIDE)], pictures.at[pl.ds(0, STRIDE)], sem
    )
    body_copy.start()

    tables[0].wait()
    lines = bank_lines(taps[...], TAPS // 2)
    for kernel in range(taps.shape[0]):
        main, edge = banded_pair(lines[kernel : kernel + 1])
        edge = edge.T
        early = lax.broadcasted_iota(jnp.int32, edge.shape, 0) < BAND_COLS // 2
        before = jnp.where(early, 0.0, edge)
        after = jnp.where(early, edge, 0.0)
        for index, part in enumerate((before, main.T, after)):
            bank_h[kernel, index * BAND_COLS : (index + 1) * BAND_COLS] = part.astype(jnp.bfloat16)
    for copy in tables[1:]:
        copy.wait()

    first_out = sky_place * rows + place * rows_out
    out_row = first_out + lax.broadcasted_iota(jnp.int32, (rows_out, exposures_total), 0)
    covered = (out_row >= range_ref[0:1, :]) & (out_row < range_ref[1:2, :])
    for band in range(bands):
        both = covered & (bad_ref[band : band + 1, :] == 0)
        number = jnp.sum(both.astype(jnp.float32), axis=1, keepdims=True)
        count_ref[:, band * BAND_COLS : (band + 1) * BAND_COLS] = jnp.broadcast_to(
            number.astype(jnp.int32), (rows_out, BAND_COLS)
        )
    body_copy.wait()


def prepare(rows_out, exposures, slot_ids, choice, bad, span, flux, horiz):
    columns = exposures.shape[2]
    kernels = horiz.shape[0]
    bands = columns // BAND_COLS
    tables = [jax.ShapeDtypeStruct(t.shape, t.dtype) for t in (slot_ids, choice, bad, span, flux)]
    hbm = pl.BlockSpec(memory_space=pltpu.HBM)
    vmem = pl.BlockSpec(memory_space=pltpu.VMEM)
    return pl.pallas_call(
        functools.partial(prepare_kernel, bands, rows_out),
        out_shape=[
            jax.ShapeDtypeStruct(exposures.shape, jnp.bfloat16),
            jax.ShapeDtypeStruct((kernels, 3 * BAND_COLS, BAND_COLS), jnp.bfloat16),
            jax.ShapeDtypeStruct((rows_out, columns), jnp.int32),
        ]
        + tables,
        in_specs=[hbm] * 7,
        out_specs=[vmem] * 8,
        scratch_shapes=[
            pltpu.VMEM(horiz.shape, jnp.bfloat16),
            pltpu.SemaphoreType.DMA,
            pltpu.SemaphoreType.DMA((6,)),
        ],
        compiler_params=pltpu.CompilerParams(vmem_limit_bytes=KERNEL_VMEM),
        cost_estimate=pl.CostEstimate(flops=1 << 20, bytes_accessed=4 << 20, transcendentals=0),
        name="prepare",
    )(
        *[
            pltpu.with_memory_space_constraint(value, pltpu.HBM)
            for value in (exposures, slot_ids, choice, bad, span, flux, horiz)
        ]
    )


def select_chunk(top, high, low, total, outs):
    slots, _, columns = high.shape
    windows = [pl.ds(start, BAND_COLS) for start in range(0, columns, BAND_COLS)]
    streams = [(w, source, up) for w in windows for source, up in ((high, True), (low, False))]
    best = [None] * len(streams)
    for piece in range(slots // REJECT):
        for n, (window, source, up) in enumerate(streams):
            entries = [
                source[piece * REJECT + i, pl.ds(top, TILE_ROWS), window] for i in range(REJECT)
            ]
            entries = sorted_four(entries, up)
            best[n] = entries if best[n] is None else merged_four(best[n], entries, up)
    bands_each = len(windows) // len(outs)
    for n, window in enumerate(windows):
        sides = best[2 * n : 2 * n + 2]
        left = total[pl.ds(top, TILE_ROWS), window] - extremes_sum(*sides)
        out = outs[n // bands_each]
        place = pl.ds((n % bands_each) * BAND_COLS, BAND_COLS)
        for index, value in enumerate(sides[0] + sides[1]):
            out[index, :, place] = value
        out[2 * REJECT, :, place] = left.astype(jnp.bfloat16)


def select_chunks(chunk_of, parts, high, low, total, outs):
    place = lax.axis_index("expo")
    for position in range(len(outs) // parts):
        top = pl.multiple_of(chunk_of(place, position) * TILE_ROWS, TILE_ROWS)
        select_chunk(top, high, low, total, outs[position * parts : (position + 1) * parts])


def filter_kernel(
    chunk_of,
    parts,
    exposures_ref,
    _,
    halo,
    bank_v,
    bank_h,
    slot_vmem,
    choice_vmem,
    bad_vmem,
    range_vmem,
    flux_vmem,
    pictures,
    high,
    low,
    total,
    *rest,
):
    *outs, slot_ref, choice_ref, bad_ref, range_ref, flux_ref, sems, body_sems = rest
    slots, rows, columns = pictures.shape
    bands = columns // BAND_COLS
    exposures_total = range_vmem.shape[1]
    place = lax.axis_index("expo")
    sky_place = lax.axis_index("sky")
    tables = [
        pltpu.make_async_copy(source, target, sems.at[i])
        for i, (source, target) in enumerate(
            (
                (slot_vmem, slot_ref),
                (choice_vmem, choice_ref),
                (bad_vmem, bad_ref),
                (range_vmem, range_ref),
                (flux_vmem, flux_ref),
            )
        )
    ]
    for copy in tables:
        copy.start()

    def body_copy(step):
        window = pl.ds(step * STRIDE, STRIDE)
        return pltpu.make_async_copy(
            exposures_ref.at[window], pictures.at[window], body_sems.at[step]
        )

    for step in range(1, slots // STRIDE):
        body_copy(step).start()
    total[...] = jnp.zeros_like(total)
    for copy in tables:
        copy.wait()

    row_index = lax.broadcasted_iota(jnp.int32, (rows, BAND_COLS), 0)
    row_index = (row_index + sky_place * rows).astype(jnp.float32).astype(jnp.bfloat16)
    zero = jnp.zeros((), jnp.bfloat16)
    sentinel = jnp.asarray(SENTINEL, jnp.bfloat16)
    lane = lax.broadcasted_iota(jnp.int32, (rows, BAND_COLS), 1)

    def first_pass(slot):
        ident = slot_ref[place, slot]
        k = jnp.minimum(ident, exposures_total - 1)
        begin = range_ref[0, k]
        end = jnp.where(ident < exposures_total, range_ref[1, k], 0)
        factor = flux_ref[k]
        chosen = [choice_ref[band, k] for band in range(bands)]
        verticals = []
        for band in range(bands):
            window = pl.ds(band * BAND_COLS, BAND_COLS)
            picture = jnp.concatenate([pictures[slot, :, window], halo[slot, :, window]], 0)
            vertical = jnp.dot(bank_v[chosen[band]], picture, preferred_element_type=jnp.float32)
            verticals.append(vertical.astype(jnp.bfloat16))
        return k, factor, chosen, begin, end, verticals

    def second_pass(slot, k, factor, chosen, begin, end, verticals):
        filtered = []
        for band in range(0, bands, 2):
            pair = jnp.dot(
                jnp.concatenate(verticals[band : band + 2], 1),
                jnp.concatenate(
                    [bank_h[chosen[band], BAND_COLS:], bank_h[chosen[band + 1], : 2 * BAND_COLS]], 1
                ),
                preferred_element_type=jnp.float32,
            )
            filtered += [pair[:, :BAND_COLS], pair[:, BAND_COLS:]]
        for band in range(2, bands, 2):
            seam = jnp.dot(
                jnp.where(lane < BAND_COLS // 2, verticals[band], verticals[band - 1]),
                jnp.concatenate(
                    [
                        bank_h[chosen[band - 1], 2 * BAND_COLS :],
                        bank_h[chosen[band], :BAND_COLS],
                    ],
                    1,
                ),
                preferred_element_type=jnp.float32,
            )
            filtered[band - 1] += seam[:, :BAND_COLS]
            filtered[band] += seam[:, BAND_COLS:]
        first_row = begin.astype(jnp.float32).astype(jnp.bfloat16)
        for band in range(bands):
            plane = (filtered[band] * factor).astype(jnp.bfloat16)
            stop = jnp.where(bad_ref[band, k] == 0, end, 0).astype(jnp.float32)
            usable = (row_index >= first_row) & (row_index < stop.astype(jnp.bfloat16))
            window = pl.ds(band * BAND_COLS, BAND_COLS)
            total[:, window] += jnp.where(usable, plane, zero).astype(jnp.float32)
            high[slot, :, window] = jnp.where(usable, plane, -sentinel)
            low[slot, :, window] = jnp.where(usable, plane, sentinel)

    def body(step, carry):
        @pl.when(step > 0)
        def _():
            body_copy(step).wait()

        held = first_pass(STRIDE * step)
        for i in range(STRIDE):
            ahead = first_pass(STRIDE * step + i + 1) if i + 1 < STRIDE else None
            second_pass(STRIDE * step + i, *held)
            held = ahead
        return carry

    lax.fori_loop(0, slots // STRIDE, body, 0)
    select_chunks(chunk_of, parts, high, low, total, outs)


def filter_slots(chunk_of, chunks, parts, exposures, pictures, halo, bank_v, bank_h, tables):
    slots, rows, columns = pictures.shape
    vmem = pl.BlockSpec(memory_space=pltpu.VMEM)
    return pl.pallas_call(
        functools.partial(filter_kernel, chunk_of, parts),
        out_shape=[
            jax.ShapeDtypeStruct(pictures.shape, jnp.bfloat16),
            jax.ShapeDtypeStruct(pictures.shape, jnp.bfloat16),
            jax.ShapeDtypeStruct(pictures.shape, jnp.bfloat16),
            jax.ShapeDtypeStruct((rows, columns), jnp.float32),
        ]
        + [jax.ShapeDtypeStruct((LISTS, TILE_ROWS, columns // parts), jnp.bfloat16)]
        * (chunks * parts),
        in_specs=[pl.BlockSpec(memory_space=pltpu.HBM)] + [vmem] * (4 + len(tables)),
        out_specs=[vmem] * (4 + chunks * parts),
        input_output_aliases={1: 0},
        scratch_shapes=[pltpu.SMEM(table.shape, table.dtype) for table in tables]
        + [
            pltpu.SemaphoreType.DMA((len(tables),)),
            pltpu.SemaphoreType.DMA((slots // STRIDE,)),
        ],
        compiler_params=pltpu.CompilerParams(vmem_limit_bytes=KERNEL_VMEM),
        cost_estimate=pl.CostEstimate(
            flops=4 * slots * rows * columns * 256, bytes_accessed=8 << 20, transcendentals=0
        ),
        name="filter_slots",
    )(
        pltpu.with_memory_space_constraint(exposures, pltpu.HBM),
        *[
            pltpu.with_memory_space_constraint(value, pltpu.VMEM)
            for value in (pictures, halo, bank_v, bank_h, *tables)
        ],
    )[1:]


def select_kernel(chunk_of, parts, high, low, total, *outs):
    select_chunks(chunk_of, parts, high, low, total, outs)


def select(chunk_of, chunks, parts, high, low, total):
    vmem = pl.BlockSpec(memory_space=pltpu.VMEM)
    return pl.pallas_call(
        functools.partial(select_kernel, chunk_of, parts),
        out_shape=[
            jax.ShapeDtypeStruct((LISTS, TILE_ROWS, high.shape[2] // parts), jnp.bfloat16)
        ]
        * (chunks * parts),
        in_specs=[vmem] * 3,
        out_specs=[vmem] * (chunks * parts),
        compiler_params=pltpu.CompilerParams(vmem_limit_bytes=KERNEL_VMEM),
        cost_estimate=pl.CostEstimate(flops=1 << 24, bytes_accessed=4 << 20, transcendentals=0),
        name="select_rows",
    )(*[pltpu.with_memory_space_constraint(value, pltpu.VMEM) for value in (high, low, total)])


def merged_lists(sources, ordered):
    sides = []
    for base, up in ((0, True), (REJECT, False)):
        lists = [[ref[base + i, :, window] for i in range(REJECT)] for ref, window in sources]
        while len(lists) > 1:
            keep = ordered or len(lists) > 2
            paired = [
                merged_four(lists[i], lists[i + 1], up, keep)
                for i in range(0, len(lists) - 1, 2)
            ]
            lists = paired + (lists[-1:] if len(lists) % 2 else [])
        sides.append(lists[0])
    grand = None
    for ref, window in sources:
        part = ref[2 * REJECT, :, window].astype(jnp.float32) + extremes_sum(
            [ref[i, :, window] for i in range(REJECT)],
            [ref[REJECT + i, :, window] for i in range(REJECT)],
        )
        grand = part if grand is None else grand + part
    return sides, grand


def merge_kernel(*refs):
    *sources, out = refs
    for band in range(out.shape[-1] // BAND_COLS):
        window = pl.ds(band * BAND_COLS, BAND_COLS)
        sides, grand = merged_lists([(ref, window) for ref in sources], True)
        for index, value in enumerate(sides[0] + sides[1]):
            out[index, :, window] = value
        out[2 * REJECT, :, window] = (grand - extremes_sum(*sides)).astype(jnp.bfloat16)


def merge(parts):
    vmem = pl.BlockSpec(memory_space=pltpu.VMEM)
    return pl.pallas_call(
        merge_kernel,
        out_shape=jax.ShapeDtypeStruct(parts[0].shape, jnp.bfloat16),
        in_specs=[vmem] * len(parts),
        out_specs=vmem,
        compiler_params=pltpu.CompilerParams(vmem_limit_bytes=KERNEL_VMEM),
        name="merge_lists",
    )(*parts)


def finish_kernel(exposures_total, whole, *refs):
    *sources, count_ref, coadd_ref, rejected_ref = refs
    whole, parts = sources[:whole], sources[whole:]
    for band in range(coadd_ref.shape[-1] // BAND_COLS):
        window = pl.ds(band * BAND_COLS, BAND_COLS)
        here = [(ref, window) for ref in whole]
        for index, ref in enumerate(parts):
            first, held = index * ref.shape[-1], ref.shape[-1]
            if first <= band * BAND_COLS < first + held:
                here.append((ref, pl.ds(band * BAND_COLS - first, BAND_COLS)))
        sides, grand = merged_lists(here, False)
        extremes = extremes_sum(*sides)
        count = count_ref[:, window]
        clipped = count >= MIN_VALID
        used = jnp.where(clipped, count - 2 * REJECT, count)
        kept = jnp.where(clipped, grand - extremes, grand)
        coadd_ref[:, window] = kept / jnp.maximum(used, 1).astype(jnp.float32)
        rejected_ref[:, window] = exposures_total - used


def finish(whole, parts, count, exposures_total):
    vmem = pl.BlockSpec(memory_space=pltpu.VMEM)
    return pl.pallas_call(
        functools.partial(finish_kernel, exposures_total, len(whole)),
        out_shape=[
            jax.ShapeDtypeStruct(count.shape, jnp.float32),
            jax.ShapeDtypeStruct(count.shape, jnp.int32),
        ],
        in_specs=[vmem] * (len(whole) + len(parts) + 1),
        out_specs=[vmem, vmem],
        compiler_params=pltpu.CompilerParams(vmem_limit_bytes=KERNEL_VMEM),
        name="finish_pixels",
    )(*whole, *parts, count)


def swapped(value, axis, distance):
    count = lax.axis_size(axis)
    return lax.ppermute(value, axis, [(i, i ^ distance) for i in range(count)])


def shards(
    exposures, slot_ids, row_range, bad_bands, kernel_choice, flux_scale, vert_taps, horiz_taps
):
    slot_count, row_dev, columns = exposures.shape
    exposures_total = flux_scale.shape[0]
    expo_size = lax.axis_size("expo")
    rows_out = row_dev // expo_size

    edges, bank_v = window_edges(exposures, vert_taps)
    halo = swapped(edges, "sky", 1)
    pictures, bank_h, count, *tables = prepare(
        rows_out,
        exposures,
        slot_ids,
        kernel_choice.T,
        bad_bands.T,
        row_range.T,
        flux_scale,
        horiz_taps,
    )

    if rows_out == TILE_ROWS and expo_size == 2 * SQUARE:
        high, low, total, *far = filter_slots(
            lambda place, i: place ^ i ^ SQUARE,
            SQUARE,
            FAR_PARTS,
            exposures,
            pictures,
            halo,
            bank_v,
            bank_h,
            tables,
        )
        across = []
        for part in range(FAR_PARTS):
            own, *sent = far[part::FAR_PARTS]
            got = [swapped(sent[i], "expo", 1 + i) for i in reversed(range(SQUARE - 1))]
            across.append(swapped(merge([own] + got), "expo", SQUARE))
        near = list(select(lambda place, i: place ^ i, SQUARE, 1, high, low, total))
        near = near[:1] + [swapped(part, "expo", 1 + i) for i, part in enumerate(near[1:])]
        coadd_plane, rejected_count = finish(near, across, count, exposures_total)
    else:
        chunks = row_dev // TILE_ROWS
        high, low, total, *lists = filter_slots(
            lambda place, i: i, chunks, 1, exposures, pictures, halo, bank_v, bank_h, tables
        )
        whole = jnp.concatenate(lists, 1)
        arrived = lax.all_to_all(whole, "expo", split_axis=1, concat_axis=0, tiled=True)
        arrived = arrived.reshape(expo_size, LISTS, rows_out, columns)
        coadd_plane, rejected_count = finish(
            [arrived[i] for i in range(expo_size)], [], count, exposures_total
        )
    return (coadd_plane[None], rejected_count[None])


def solution(mesh):
    in_specs = (
        P(("groups", "expo"), "sky", None),
        P("groups", None),
        P("groups", None),
        P("groups", None),
        P("groups", None),
        P("groups"),
        P("groups", None),
        P("groups", None),
    )
    out_specs = (P(("groups", "sky"), "expo", None), P(("groups", "sky"), "expo", None))
    return jax.shard_map(shards, mesh=mesh, in_specs=in_specs, out_specs=out_specs, check_vma=False)
```

```python
import functools

import jax
import jax.numpy as jnp
from jax import lax
from jax.experimental import pallas as pl
from jax.experimental.pallas import tpu as pltpu
from jax.sharding import PartitionSpec as P

BAND_COLS = 128
TAPS = 21
REJECT = 4
MIN_VALID = 12

SENTINEL = 1e30

TILE_ROWS = 16
PAD = 16
STRIDE = 8
FAR_PARTS = 1
SQUARE = 4
KERNEL_VMEM = 8 * 1024 * 1024
LISTS = 2 * REJECT + 1


def sort_pair(entries, first, second, up):
    a, b = entries[first], entries[second]
    hi, lo = jnp.maximum(a, b), jnp.minimum(a, b)
    entries[first], entries[second] = (hi, lo) if up else (lo, hi)


def sorted_four(entries, up):
    entries = list(entries)
    for first, second in ((0, 1), (2, 3), (0, 2), (1, 3), (1, 2)):
        sort_pair(entries, first, second, up)
    return entries


def merged_four(left, right, up, ordered=True):
    pick = jnp.maximum if up else jnp.minimum
    entries = [pick(left[i], right[REJECT - 1 - i]) for i in range(REJECT)]
    if ordered:
        for first, second in ((0, 2), (1, 3), (0, 1), (2, 3)):
            sort_pair(entries, first, second, up)
    return entries


def extremes_sum(highs, lows):
    pairs = [h.astype(jnp.float32) + l.astype(jnp.float32) for h, l in zip(highs, lows, strict=True)]
    return functools.reduce(jnp.add, pairs)


def banded_pair(line):
    offset = lax.broadcasted_iota(jnp.int32, (BAND_COLS, BAND_COLS), 1) - (
        lax.broadcasted_iota(jnp.int32, (BAND_COLS, BAND_COLS), 0)
    )
    inside = jnp.abs(offset) < BAND_COLS // 2
    banded = pltpu.roll(
        jnp.broadcast_to(line, (BAND_COLS, BAND_COLS)), 0, 1, stride=1, stride_axis=0
    )
    return jnp.where(inside, banded, 0.0), jnp.where(inside, 0.0, banded)


def bank_lines(taps, margin):
    lines = jnp.pad(taps.astype(jnp.float32), ((0, 0), (0, BAND_COLS - TAPS)))
    return pltpu.roll(lines, BAND_COLS - margin, 1)


def edge_kernel(exposures_ref, vert_hbm, edge_ref, bank_v, taps, sems):
    rows = exposures_ref.shape[1]
    sky_place = lax.axis_index("sky")
    start = pl.multiple_of((1 - sky_place) * (rows - PAD), TILE_ROWS)
    edge_copy = pltpu.make_async_copy(
        exposures_ref.at[:, pl.ds(start, PAD), :], edge_ref, sems.at[0]
    )
    taps_copy = pltpu.make_async_copy(vert_hbm, taps, sems.at[1])
    taps_copy.start()
    edge_copy.start()
    taps_copy.wait()
    lines = bank_lines(taps[...], TAPS // 2)
    turn = PAD * sky_place
    for kernel in range(taps.shape[0]):
        main, edge = banded_pair(lines[kernel : kernel + 1])
        bank_v[kernel, :, :BAND_COLS] = main.astype(jnp.bfloat16)
        bank_v[kernel, :, BAND_COLS:] = pltpu.roll(edge, turn, 1)[:, :PAD].astype(jnp.bfloat16)
    edge_copy.wait()


def window_edges(exposures, vert):
    slots, rows, columns = exposures.shape
    hbm = pl.BlockSpec(memory_space=pltpu.HBM)
    vmem = pl.BlockSpec(memory_space=pltpu.VMEM)
    return pl.pallas_call(
        edge_kernel,
        out_shape=[
            jax.ShapeDtypeStruct((slots, PAD, columns), jnp.bfloat16),
            jax.ShapeDtypeStruct((vert.shape[0], rows, BAND_COLS + PAD), jnp.bfloat16),
        ],
        in_specs=[hbm] * 2,
        out_specs=[vmem] * 2,
        scratch_shapes=[pltpu.VMEM(vert.shape, jnp.bfloat16), pltpu.SemaphoreType.DMA((2,))],
        compiler_params=pltpu.CompilerParams(vmem_limit_bytes=KERNEL_VMEM),
        name="window_edges",
    )(*[pltpu.with_memory_space_constraint(value, pltpu.HBM) for value in (exposures, vert)])


def prepare_kernel(
    bands,
    rows_out,
    exposures_ref,
    slot_hbm,
    choice_hbm,
    bad_hbm,
    range_hbm,
    flux_hbm,
    horiz_hbm,
    pictures,
    bank_h,
    count_ref,
    slot_ref,
    choice_ref,
    bad_ref,
    range_ref,
    flux_ref,
    taps,
    sem,
    table_sems,
):
    rows = exposures_ref.shape[1]
    exposures_total = range_ref.shape[1]
    place = lax.axis_index("expo")
    sky_place = lax.axis_index("sky")
    tables = [
        pltpu.make_async_copy(source, target, table_sems.at[i])
        for i, (source, target) in enumerate(
            (
                (horiz_hbm, taps),
                (slot_hbm, slot_ref),
                (choice_hbm, choice_ref),
                (bad_hbm, bad_ref),
                (range_hbm, range_ref),
                (flux_hbm, flux_ref),
            )
        )
    ]
    for copy in tables:
        copy.start()
    body_copy = pltpu.make_async_copy(
        exposures_ref.at[pl.ds(0, STRIDE)], pictures.at[pl.ds(0, STRIDE)], sem
    )
    body_copy.start()

    tables[0].wait()
    lines = bank_lines(taps[...], TAPS // 2)
    for kernel in range(taps.shape[0]):
        main, edge = banded_pair(lines[kernel : kernel + 1])
        edge = edge.T
        early = lax.broadcasted_iota(jnp.int32, edge.shape, 0) < BAND_COLS // 2
        before = jnp.where(early, 0.0, edge)
        after = jnp.where(early, edge, 0.0)
        for index, part in enumerate((before, main.T, after)):
            bank_h[kernel, index * BAND_COLS : (index + 1) * BAND_COLS] = part.astype(jnp.bfloat16)
    for copy in tables[1:]:
        copy.wait()

    first_out = sky_place * rows + place * rows_out
    out_row = first_out + lax.broadcasted_iota(jnp.int32, (rows_out, exposures_total), 0)
    covered = (out_row >= range_ref[0:1, :]) & (out_row < range_ref[1:2, :])
    for band in range(bands):
        both = covered & (bad_ref[band : band + 1, :] == 0)
        number = jnp.sum(both.astype(jnp.float32), axis=1, keepdims=True)
        count_ref[:, band * BAND_COLS : (band + 1) * BAND_COLS] = jnp.broadcast_to(
            number.astype(jnp.int32), (rows_out, BAND_COLS)
        )
    body_copy.wait()


def prepare(rows_out, exposures, slot_ids, choice, bad, span, flux, horiz):
    columns = exposures.shape[2]
    kernels = horiz.shape[0]
    bands = columns // BAND_COLS
    tables = [jax.ShapeDtypeStruct(t.shape, t.dtype) for t in (slot_ids, choice, bad, span, flux)]
    hbm = pl.BlockSpec(memory_space=pltpu.HBM)
    vmem = pl.BlockSpec(memory_space=pltpu.VMEM)
    return pl.pallas_call(
        functools.partial(prepare_kernel, bands, rows_out),
        out_shape=[
            jax.ShapeDtypeStruct(exposures.shape, jnp.bfloat16),
            jax.ShapeDtypeStruct((kernels, 3 * BAND_COLS, BAND_COLS), jnp.bfloat16),
            jax.ShapeDtypeStruct((rows_out, columns), jnp.int32),
        ]
        + tables,
        in_specs=[hbm] * 7,
        out_specs=[vmem] * 8,
        scratch_shapes=[
            pltpu.VMEM(horiz.shape, jnp.bfloat16),
            pltpu.SemaphoreType.DMA,
            pltpu.SemaphoreType.DMA((6,)),
        ],
        compiler_params=pltpu.CompilerParams(vmem_limit_bytes=KERNEL_VMEM),
        cost_estimate=pl.CostEstimate(flops=1 << 20, bytes_accessed=4 << 20, transcendentals=0),
        name="prepare",
    )(
        *[
            pltpu.with_memory_space_constraint(value, pltpu.HBM)
            for value in (exposures, slot_ids, choice, bad, span, flux, horiz)
        ]
    )


def select_chunk(top, high, low, total, outs):
    slots, _, columns = high.shape
    windows = [pl.ds(start, BAND_COLS) for start in range(0, columns, BAND_COLS)]
    streams = [(w, source, up) for w in windows for source, up in ((high, True), (low, False))]
    best = [None] * len(streams)
    for piece in range(slots // REJECT):
        for n, (window, source, up) in enumerate(streams):
            entries = [
                source[piece * REJECT + i, pl.ds(top, TILE_ROWS), window] for i in range(REJECT)
            ]
            entries = sorted_four(entries, up)
            best[n] = entries if best[n] is None else merged_four(best[n], entries, up)
    bands_each = len(windows) // len(outs)
    for n, window in enumerate(windows):
        sides = best[2 * n : 2 * n + 2]
        left = total[pl.ds(top, TILE_ROWS), window] - extremes_sum(*sides)
        out = outs[n // bands_each]
        place = pl.ds((n % bands_each) * BAND_COLS, BAND_COLS)
        for index, value in enumerate(sides[0] + sides[1]):
            out[index, :, place] = value
        out[2 * REJECT, :, place] = left.astype(jnp.bfloat16)


def select_chunks(chunk_of, parts, high, low, total, outs):
    place = lax.axis_index("expo")
    for position in range(len(outs) // parts):
        top = pl.multiple_of(chunk_of(place, position) * TILE_ROWS, TILE_ROWS)
        select_chunk(top, high, low, total, outs[position * parts : (position + 1) * parts])


def filter_kernel(
    chunk_of,
    parts,
    exposures_ref,
    _,
    halo,
    bank_v,
    bank_h,
    slot_vmem,
    choice_vmem,
    bad_vmem,
    range_vmem,
    flux_vmem,
    pictures,
    high,
    low,
    total,
    *rest,
):
    *outs, slot_ref, choice_ref, bad_ref, range_ref, flux_ref, sems, body_sems = rest
    slots, rows, columns = pictures.shape
    bands = columns // BAND_COLS
    exposures_total = range_vmem.shape[1]
    place = lax.axis_index("expo")
    sky_place = lax.axis_index("sky")
    tables = [
        pltpu.make_async_copy(source, target, sems.at[i])
        for i, (source, target) in enumerate(
            (
                (slot_vmem, slot_ref),
                (choice_vmem, choice_ref),
                (bad_vmem, bad_ref),
                (range_vmem, range_ref),
                (flux_vmem, flux_ref),
            )
        )
    ]
    for copy in tables:
        copy.start()

    def body_copy(step):
        window = pl.ds(step * STRIDE, STRIDE)
        return pltpu.make_async_copy(
            exposures_ref.at[window], pictures.at[window], body_sems.at[step]
        )

    for step in range(1, slots // STRIDE):
        body_copy(step).start()
    total[...] = jnp.zeros_like(total)
    for copy in tables:
        copy.wait()

    row_index = lax.broadcasted_iota(jnp.int32, (rows, BAND_COLS), 0)
    row_index = (row_index + sky_place * rows).astype(jnp.float32).astype(jnp.bfloat16)
    zero = jnp.zeros((), jnp.bfloat16)
    sentinel = jnp.asarray(SENTINEL, jnp.bfloat16)
    lane = lax.broadcasted_iota(jnp.int32, (rows, BAND_COLS), 1)

    def first_pass(slot):
        ident = slot_ref[place, slot]
        k = jnp.minimum(ident, exposures_total - 1)
        begin = range_ref[0, k]
        end = jnp.where(ident < exposures_total, range_ref[1, k], 0)
        factor = flux_ref[k]
        chosen = [choice_ref[band, k] for band in range(bands)]
        verticals = []
        for band in range(bands):
            window = pl.ds(band * BAND_COLS, BAND_COLS)
            picture = jnp.concatenate([pictures[slot, :, window], halo[slot, :, window]], 0)
            vertical = jnp.dot(bank_v[chosen[band]], picture, preferred_element_type=jnp.float32)
            verticals.append(vertical.astype(jnp.bfloat16))
        return k, factor, chosen, begin, end, verticals

    def second_pass(slot, k, factor, chosen, begin, end, verticals):
        filtered = []
        for band in range(0, bands, 2):
            pair = jnp.dot(
                jnp.concatenate(verticals[band : band + 2], 1),
                jnp.concatenate(
                    [bank_h[chosen[band], BAND_COLS:], bank_h[chosen[band + 1], : 2 * BAND_COLS]], 1
                ),
                preferred_element_type=jnp.float32,
            )
            filtered += [pair[:, :BAND_COLS], pair[:, BAND_COLS:]]
        for band in range(2, bands, 2):
            seam = jnp.dot(
                jnp.where(lane < BAND_COLS // 2, verticals[band], verticals[band - 1]),
                jnp.concatenate(
                    [
                        bank_h[chosen[band - 1], 2 * BAND_COLS :],
                        bank_h[chosen[band], :BAND_COLS],
                    ],
                    1,
                ),
                preferred_element_type=jnp.float32,
            )
            filtered[band - 1] += seam[:, :BAND_COLS]
            filtered[band] += seam[:, BAND_COLS:]
        first_row = begin.astype(jnp.float32).astype(jnp.bfloat16)
        for band in range(bands):
            plane = (filtered[band] * factor).astype(jnp.bfloat16)
            stop = jnp.where(bad_ref[band, k] == 0, end, 0).astype(jnp.float32)
            usable = (row_index >= first_row) & (row_index < stop.astype(jnp.bfloat16))
            window = pl.ds(band * BAND_COLS, BAND_COLS)
            total[:, window] += jnp.where(usable, plane, zero).astype(jnp.float32)
            high[slot, :, window] = jnp.where(usable, plane, -sentinel)
            low[slot, :, window] = jnp.where(usable, plane, sentinel)

    def body(step, carry):
        @pl.when(step > 0)
        def _():
            body_copy(step).wait()

        held = first_pass(STRIDE * step)
        for i in range(STRIDE):
            ahead = first_pass(STRIDE * step + i + 1) if i + 1 < STRIDE else None
            second_pass(STRIDE * step + i, *held)
            held = ahead
        return carry

    lax.fori_loop(0, slots // STRIDE, body, 0)
    select_chunks(chunk_of, parts, high, low, total, outs)


def filter_slots(chunk_of, chunks, parts, exposures, pictures, halo, bank_v, bank_h, tables):
    slots, rows, columns = pictures.shape
    vmem = pl.BlockSpec(memory_space=pltpu.VMEM)
    return pl.pallas_call(
        functools.partial(filter_kernel, chunk_of, parts),
        out_shape=[
            jax.ShapeDtypeStruct(pictures.shape, jnp.bfloat16),
            jax.ShapeDtypeStruct(pictures.shape, jnp.bfloat16),
            jax.ShapeDtypeStruct(pictures.shape, jnp.bfloat16),
            jax.ShapeDtypeStruct((rows, columns), jnp.float32),
        ]
        + [jax.ShapeDtypeStruct((LISTS, TILE_ROWS, columns // parts), jnp.bfloat16)]
        * (chunks * parts),
        in_specs=[pl.BlockSpec(memory_space=pltpu.HBM)] + [vmem] * (4 + len(tables)),
        out_specs=[vmem] * (4 + chunks * parts),
        input_output_aliases={1: 0},
        scratch_shapes=[pltpu.SMEM(table.shape, table.dtype) for table in tables]
        + [
            pltpu.SemaphoreType.DMA((len(tables),)),
            pltpu.SemaphoreType.DMA((slots // STRIDE,)),
        ],
        compiler_params=pltpu.CompilerParams(vmem_limit_bytes=KERNEL_VMEM),
        cost_estimate=pl.CostEstimate(
            flops=4 * slots * rows * columns * 256, bytes_accessed=8 << 20, transcendentals=0
        ),
        name="filter_slots",
    )(
        pltpu.with_memory_space_constraint(exposures, pltpu.HBM),
        *[
            pltpu.with_memory_space_constraint(value, pltpu.VMEM)
            for value in (pictures, halo, bank_v, bank_h, *tables)
        ],
    )[1:]


def select_kernel(chunk_of, parts, high, low, total, *outs):
    select_chunks(chunk_of, parts, high, low, total, outs)


def select(chunk_of, chunks, parts, high, low, total):
    vmem = pl.BlockSpec(memory_space=pltpu.VMEM)
    return pl.pallas_call(
        functools.partial(select_kernel, chunk_of, parts),
        out_shape=[
            jax.ShapeDtypeStruct((LISTS, TILE_ROWS, high.shape[2] // parts), jnp.bfloat16)
        ]
        * (chunks * parts),
        in_specs=[vmem] * 3,
        out_specs=[vmem] * (chunks * parts),
        compiler_params=pltpu.CompilerParams(vmem_limit_bytes=KERNEL_VMEM),
        cost_estimate=pl.CostEstimate(flops=1 << 24, bytes_accessed=4 << 20, transcendentals=0),
        name="select_rows",
    )(*[pltpu.with_memory_space_constraint(value, pltpu.VMEM) for value in (high, low, total)])


def merged_lists(sources, ordered):
    sides = []
    for base, up in ((0, True), (REJECT, False)):
        lists = [[ref[base + i, :, window] for i in range(REJECT)] for ref, window in sources]
        while len(lists) > 1:
            keep = ordered or len(lists) > 2
            paired = [
                merged_four(lists[i], lists[i + 1], up, keep)
                for i in range(0, len(lists) - 1, 2)
            ]
            lists = paired + (lists[-1:] if len(lists) % 2 else [])
        sides.append(lists[0])
    grand = None
    for ref, window in sources:
        part = ref[2 * REJECT, :, window].astype(jnp.float32) + extremes_sum(
            [ref[i, :, window] for i in range(REJECT)],
            [ref[REJECT + i, :, window] for i in range(REJECT)],
        )
        grand = part if grand is None else grand + part
    return sides, grand


def merge_kernel(*refs):
    *sources, out = refs
    for band in range(out.shape[-1] // BAND_COLS):
        window = pl.ds(band * BAND_COLS, BAND_COLS)
        sides, grand = merged_lists([(ref, window) for ref in sources], True)
        for index, value in enumerate(sides[0] + sides[1]):
            out[index, :, window] = value
        out[2 * REJECT, :, window] = (grand - extremes_sum(*sides)).astype(jnp.bfloat16)


def merge(parts):
    vmem = pl.BlockSpec(memory_space=pltpu.VMEM)
    return pl.pallas_call(
        merge_kernel,
        out_shape=jax.ShapeDtypeStruct(parts[0].shape, jnp.bfloat16),
        in_specs=[vmem] * len(parts),
        out_specs=vmem,
        compiler_params=pltpu.CompilerParams(vmem_limit_bytes=KERNEL_VMEM),
        name="merge_lists",
    )(*parts)


def finish_kernel(exposures_total, whole, *refs):
    *sources, count_ref, coadd_ref, rejected_ref = refs
    whole, parts = sources[:whole], sources[whole:]
    for band in range(coadd_ref.shape[-1] // BAND_COLS):
        window = pl.ds(band * BAND_COLS, BAND_COLS)
        here = [(ref, window) for ref in whole]
        for index, ref in enumerate(parts):
            first, held = index * ref.shape[-1], ref.shape[-1]
            if first <= band * BAND_COLS < first + held:
                here.append((ref, pl.ds(band * BAND_COLS - first, BAND_COLS)))
        sides, grand = merged_lists(here, False)
        extremes = extremes_sum(*sides)
        count = count_ref[:, window]
        clipped = count >= MIN_VALID
        used = jnp.where(clipped, count - 2 * REJECT, count)
        kept = jnp.where(clipped, grand - extremes, grand)
        coadd_ref[:, window] = kept / jnp.maximum(used, 1).astype(jnp.float32)
        rejected_ref[:, window] = exposures_total - used


def finish(whole, parts, count, exposures_total):
    vmem = pl.BlockSpec(memory_space=pltpu.VMEM)
    return pl.pallas_call(
        functools.partial(finish_kernel, exposures_total, len(whole)),
        out_shape=[
            jax.ShapeDtypeStruct(count.shape, jnp.float32),
            jax.ShapeDtypeStruct(count.shape, jnp.int32),
        ],
        in_specs=[vmem] * (len(whole) + len(parts) + 1),
        out_specs=[vmem, vmem],
        compiler_params=pltpu.CompilerParams(vmem_limit_bytes=KERNEL_VMEM),
        name="finish_pixels",
    )(*whole, *parts, count)


def swapped(value, axis, distance):
    count = lax.axis_size(axis)
    return lax.ppermute(value, axis, [(i, i ^ distance) for i in range(count)])


def shards(
    exposures, slot_ids, row_range, bad_bands, kernel_choice, flux_scale, vert_taps, horiz_taps
):
    slot_count, row_dev, columns = exposures.shape
    exposures_total = flux_scale.shape[0]
    expo_size = lax.axis_size("expo")
    rows_out = row_dev // expo_size

    edges, bank_v = window_edges(exposures, vert_taps)
    halo = swapped(edges, "sky", 1)
    pictures, bank_h, count, *tables = prepare(
        rows_out,
        exposures,
        slot_ids,
        kernel_choice.T,
        bad_bands.T,
        row_range.T,
        flux_scale,
        horiz_taps,
    )

    if rows_out == TILE_ROWS and expo_size == 2 * SQUARE:
        high, low, total, *sent = filter_slots(
            lambda place, i: place ^ (i + 1) ^ SQUARE,
            SQUARE - 1,
            1,
            exposures,
            pictures,
            halo,
            bank_v,
            bank_h,
            tables,
        )
        got = [swapped(sent[i], "expo", 1 + i) for i in reversed(range(SQUARE - 1))]
        kept, *near = select(
            lambda place, i: place ^ (SQUARE if i == 0 else i - 1),
            SQUARE + 1,
            1,
            high,
            low,
            total,
        )
        near = near[:1] + [swapped(part, "expo", 1 + i) for i, part in enumerate(near[1:])]
        across = swapped(merge([kept] + got), "expo", SQUARE)
        coadd_plane, rejected_count = finish(
            [merge(near[:-1]), near[-1], across], [], count, exposures_total
        )
    else:
        chunks = row_dev // TILE_ROWS
        high, low, total, *lists = filter_slots(
            lambda place, i: i, chunks, 1, exposures, pictures, halo, bank_v, bank_h, tables
        )
        whole = jnp.concatenate(lists, 1)
        arrived = lax.all_to_all(whole, "expo", split_axis=1, concat_axis=0, tiled=True)
        arrived = arrived.reshape(expo_size, LISTS, rows_out, columns)
        coadd_plane, rejected_count = finish(
            [arrived[i] for i in range(expo_size)], [], count, exposures_total
        )
    return (coadd_plane[None], rejected_count[None])


def solution(mesh):
    in_specs = (
        P(("groups", "expo"), "sky", None),
        P("groups", None),
        P("groups", None),
        P("groups", None),
        P("groups", None),
        P("groups"),
        P("groups", None),
        P("groups", None),
    )
    out_specs = (P(("groups", "sky"), "expo", None), P(("groups", "sky"), "expo", None))
    return jax.shard_map(shards, mesh=mesh, in_specs=in_specs, out_specs=out_specs, check_vma=False)
```

```python
import functools

import jax
import jax.numpy as jnp
from jax import lax
from jax.experimental import pallas as pl
from jax.experimental.pallas import tpu as pltpu
from jax.sharding import PartitionSpec as P

BAND_COLS = 128
TAPS = 21
REJECT = 4
MIN_VALID = 12

SENTINEL = 1e30

TILE_ROWS = 16
PAD = 16
STRIDE = 8
FAR_PARTS = 1
SQUARE = 4
KERNEL_VMEM = 8 * 1024 * 1024
LISTS = 2 * REJECT + 1


def sort_pair(entries, first, second, up):
    a, b = entries[first], entries[second]
    hi, lo = jnp.maximum(a, b), jnp.minimum(a, b)
    entries[first], entries[second] = (hi, lo) if up else (lo, hi)


def sorted_four(entries, up):
    entries = list(entries)
    for first, second in ((0, 1), (2, 3), (0, 2), (1, 3), (1, 2)):
        sort_pair(entries, first, second, up)
    return entries


def merged_four(left, right, up, ordered=True):
    pick = jnp.maximum if up else jnp.minimum
    entries = [pick(left[i], right[REJECT - 1 - i]) for i in range(REJECT)]
    if ordered:
        for first, second in ((0, 2), (1, 3), (0, 1), (2, 3)):
            sort_pair(entries, first, second, up)
    return entries


def extremes_sum(highs, lows):
    pairs = [h.astype(jnp.float32) + l.astype(jnp.float32) for h, l in zip(highs, lows, strict=True)]
    return functools.reduce(jnp.add, pairs)


def banded_pair(line):
    offset = lax.broadcasted_iota(jnp.int32, (BAND_COLS, BAND_COLS), 1) - (
        lax.broadcasted_iota(jnp.int32, (BAND_COLS, BAND_COLS), 0)
    )
    inside = jnp.abs(offset) < BAND_COLS // 2
    banded = pltpu.roll(
        jnp.broadcast_to(line, (BAND_COLS, BAND_COLS)), 0, 1, stride=1, stride_axis=0
    )
    return jnp.where(inside, banded, 0.0), jnp.where(inside, 0.0, banded)


def bank_lines(taps, margin):
    lines = jnp.pad(taps.astype(jnp.float32), ((0, 0), (0, BAND_COLS - TAPS)))
    return pltpu.roll(lines, BAND_COLS - margin, 1)


def edge_kernel(exposures_ref, vert_hbm, edge_ref, bank_v, taps, sems):
    rows = exposures_ref.shape[1]
    sky_place = lax.axis_index("sky")
    start = pl.multiple_of((1 - sky_place) * (rows - PAD), TILE_ROWS)
    edge_copy = pltpu.make_async_copy(
        exposures_ref.at[:, pl.ds(start, PAD), :], edge_ref, sems.at[0]
    )
    taps_copy = pltpu.make_async_copy(vert_hbm, taps, sems.at[1])
    taps_copy.start()
    edge_copy.start()
    taps_copy.wait()
    lines = bank_lines(taps[...], TAPS // 2)
    turn = PAD * sky_place
    for kernel in range(taps.shape[0]):
        main, edge = banded_pair(lines[kernel : kernel + 1])
        bank_v[kernel, :, :BAND_COLS] = main.astype(jnp.bfloat16)
        bank_v[kernel, :, BAND_COLS:] = pltpu.roll(edge, turn, 1)[:, :PAD].astype(jnp.bfloat16)
    edge_copy.wait()


def window_edges(exposures, vert):
    slots, rows, columns = exposures.shape
    hbm = pl.BlockSpec(memory_space=pltpu.HBM)
    vmem = pl.BlockSpec(memory_space=pltpu.VMEM)
    return pl.pallas_call(
        edge_kernel,
        out_shape=[
            jax.ShapeDtypeStruct((slots, PAD, columns), jnp.bfloat16),
            jax.ShapeDtypeStruct((vert.shape[0], rows, BAND_COLS + PAD), jnp.bfloat16),
        ],
        in_specs=[hbm] * 2,
        out_specs=[vmem] * 2,
        scratch_shapes=[pltpu.VMEM(vert.shape, jnp.bfloat16), pltpu.SemaphoreType.DMA((2,))],
        compiler_params=pltpu.CompilerParams(vmem_limit_bytes=KERNEL_VMEM),
        name="window_edges",
    )(*[pltpu.with_memory_space_constraint(value, pltpu.HBM) for value in (exposures, vert)])


def prepare_kernel(
    bands,
    rows_out,
    exposures_ref,
    slot_hbm,
    choice_hbm,
    bad_hbm,
    range_hbm,
    flux_hbm,
    horiz_hbm,
    pictures,
    bank_h,
    count_ref,
    slot_ref,
    choice_ref,
    bad_ref,
    range_ref,
    flux_ref,
    taps,
    sem,
    table_sems,
):
    rows = exposures_ref.shape[1]
    exposures_total = range_ref.shape[1]
    place = lax.axis_index("expo")
    sky_place = lax.axis_index("sky")
    tables = [
        pltpu.make_async_copy(source, target, table_sems.at[i])
        for i, (source, target) in enumerate(
            (
                (horiz_hbm, taps),
                (slot_hbm, slot_ref),
                (choice_hbm, choice_ref),
                (bad_hbm, bad_ref),
                (range_hbm, range_ref),
                (flux_hbm, flux_ref),
            )
        )
    ]
    for copy in tables:
        copy.start()
    body_copy = pltpu.make_async_copy(
        exposures_ref.at[pl.ds(0, STRIDE)], pictures.at[pl.ds(0, STRIDE)], sem
    )
    body_copy.start()

    tables[0].wait()
    lines = bank_lines(taps[...], TAPS // 2)
    for kernel in range(taps.shape[0]):
        main, edge = banded_pair(lines[kernel : kernel + 1])
        edge = edge.T
        early = lax.broadcasted_iota(jnp.int32, edge.shape, 0) < BAND_COLS // 2
        before = jnp.where(early, 0.0, edge)
        after = jnp.where(early, edge, 0.0)
        for index, part in enumerate((before, main.T, after)):
            bank_h[kernel, index * BAND_COLS : (index + 1) * BAND_COLS] = part.astype(jnp.bfloat16)
    for copy in tables[1:]:
        copy.wait()

    first_out = sky_place * rows + place * rows_out
    out_row = first_out + lax.broadcasted_iota(jnp.int32, (rows_out, exposures_total), 0)
    covered = (out_row >= range_ref[0:1, :]) & (out_row < range_ref[1:2, :])
    for band in range(bands):
        both = covered & (bad_ref[band : band + 1, :] == 0)
        number = jnp.sum(both.astype(jnp.float32), axis=1, keepdims=True)
        count_ref[:, band * BAND_COLS : (band + 1) * BAND_COLS] = jnp.broadcast_to(
            number.astype(jnp.int32), (rows_out, BAND_COLS)
        )
    body_copy.wait()


def prepare(rows_out, exposures, slot_ids, choice, bad, span, flux, horiz):
    columns = exposures.shape[2]
    kernels = horiz.shape[0]
    bands = columns // BAND_COLS
    tables = [jax.ShapeDtypeStruct(t.shape, t.dtype) for t in (slot_ids, choice, bad, span, flux)]
    hbm = pl.BlockSpec(memory_space=pltpu.HBM)
    vmem = pl.BlockSpec(memory_space=pltpu.VMEM)
    return pl.pallas_call(
        functools.partial(prepare_kernel, bands, rows_out),
        out_shape=[
            jax.ShapeDtypeStruct(exposures.shape, jnp.bfloat16),
            jax.ShapeDtypeStruct((kernels, 3 * BAND_COLS, BAND_COLS), jnp.bfloat16),
            jax.ShapeDtypeStruct((rows_out, columns), jnp.int32),
        ]
        + tables,
        in_specs=[hbm] * 7,
        out_specs=[vmem] * 8,
        scratch_shapes=[
            pltpu.VMEM(horiz.shape, jnp.bfloat16),
            pltpu.SemaphoreType.DMA,
            pltpu.SemaphoreType.DMA((6,)),
        ],
        compiler_params=pltpu.CompilerParams(vmem_limit_bytes=KERNEL_VMEM),
        cost_estimate=pl.CostEstimate(flops=1 << 20, bytes_accessed=4 << 20, transcendentals=0),
        name="prepare",
    )(
        *[
            pltpu.with_memory_space_constraint(value, pltpu.HBM)
            for value in (exposures, slot_ids, choice, bad, span, flux, horiz)
        ]
    )


def select_chunk(top, high, low, total, outs):
    slots, _, columns = high.shape
    windows = [pl.ds(start, BAND_COLS) for start in range(0, columns, BAND_COLS)]
    streams = [(w, source, up) for w in windows for source, up in ((high, True), (low, False))]
    best = [None] * len(streams)
    for piece in range(slots // REJECT):
        for n, (window, source, up) in enumerate(streams):
            entries = [
                source[piece * REJECT + i, pl.ds(top, TILE_ROWS), window] for i in range(REJECT)
            ]
            entries = sorted_four(entries, up)
            best[n] = entries if best[n] is None else merged_four(best[n], entries, up)
    bands_each = len(windows) // len(outs)
    for n, window in enumerate(windows):
        sides = best[2 * n : 2 * n + 2]
        left = total[pl.ds(top, TILE_ROWS), window] - extremes_sum(*sides)
        out = outs[n // bands_each]
        place = pl.ds((n % bands_each) * BAND_COLS, BAND_COLS)
        for index, value in enumerate(sides[0] + sides[1]):
            out[index, :, place] = value
        out[2 * REJECT, :, place] = left.astype(jnp.bfloat16)


def select_chunks(chunk_of, parts, high, low, total, outs):
    place = lax.axis_index("expo")
    for position in range(len(outs) // parts):
        top = pl.multiple_of(chunk_of(place, position) * TILE_ROWS, TILE_ROWS)
        select_chunk(top, high, low, total, outs[position * parts : (position + 1) * parts])


def filter_kernel(
    chunk_of,
    parts,
    exposures_ref,
    _,
    halo,
    bank_v,
    bank_h,
    slot_vmem,
    choice_vmem,
    bad_vmem,
    range_vmem,
    flux_vmem,
    pictures,
    high,
    low,
    total,
    *rest,
):
    *outs, slot_ref, choice_ref, bad_ref, range_ref, flux_ref, sems, body_sems = rest
    slots, rows, columns = pictures.shape
    bands = columns // BAND_COLS
    exposures_total = range_vmem.shape[1]
    place = lax.axis_index("expo")
    sky_place = lax.axis_index("sky")
    tables = [
        pltpu.make_async_copy(source, target, sems.at[i])
        for i, (source, target) in enumerate(
            (
                (slot_vmem, slot_ref),
                (choice_vmem, choice_ref),
                (bad_vmem, bad_ref),
                (range_vmem, range_ref),
                (flux_vmem, flux_ref),
            )
        )
    ]
    for copy in tables:
        copy.start()

    def body_copy(step):
        window = pl.ds(step * STRIDE, STRIDE)
        return pltpu.make_async_copy(
            exposures_ref.at[window], pictures.at[window], body_sems.at[step]
        )

    for step in range(1, slots // STRIDE):
        body_copy(step).start()
    total[...] = jnp.zeros_like(total)
    for copy in tables:
        copy.wait()

    row_index = lax.broadcasted_iota(jnp.int32, (rows, BAND_COLS), 0)
    row_index = (row_index + sky_place * rows).astype(jnp.float32).astype(jnp.bfloat16)
    zero = jnp.zeros((), jnp.bfloat16)
    sentinel = jnp.asarray(SENTINEL, jnp.bfloat16)
    lane = lax.broadcasted_iota(jnp.int32, (rows, BAND_COLS), 1)

    def first_pass(slot):
        ident = slot_ref[place, slot]
        k = jnp.minimum(ident, exposures_total - 1)
        begin = range_ref[0, k]
        end = jnp.where(ident < exposures_total, range_ref[1, k], 0)
        factor = flux_ref[k]
        chosen = [choice_ref[band, k] for band in range(bands)]
        verticals = []
        for band in range(bands):
            window = pl.ds(band * BAND_COLS, BAND_COLS)
            picture = jnp.concatenate([pictures[slot, :, window], halo[slot, :, window]], 0)
            vertical = jnp.dot(bank_v[chosen[band]], picture, preferred_element_type=jnp.float32)
            verticals.append(vertical.astype(jnp.bfloat16))
        return k, factor, chosen, begin, end, verticals

    def second_pass(slot, k, factor, chosen, begin, end, verticals):
        filtered = []
        for band in range(0, bands, 2):
            pair = jnp.dot(
                jnp.concatenate(verticals[band : band + 2], 1),
                jnp.concatenate(
                    [bank_h[chosen[band], BAND_COLS:], bank_h[chosen[band + 1], : 2 * BAND_COLS]], 1
                ),
                preferred_element_type=jnp.float32,
            )
            filtered += [pair[:, :BAND_COLS], pair[:, BAND_COLS:]]
        for band in range(2, bands, 2):
            seam = jnp.dot(
                jnp.where(lane < BAND_COLS // 2, verticals[band], verticals[band - 1]),
                jnp.concatenate(
                    [
                        bank_h[chosen[band - 1], 2 * BAND_COLS :],
                        bank_h[chosen[band], :BAND_COLS],
                    ],
                    1,
                ),
                preferred_element_type=jnp.float32,
            )
            filtered[band - 1] += seam[:, :BAND_COLS]
            filtered[band] += seam[:, BAND_COLS:]
        first_row = begin.astype(jnp.float32).astype(jnp.bfloat16)
        for band in range(bands):
            plane = (filtered[band] * factor).astype(jnp.bfloat16)
            stop = jnp.where(bad_ref[band, k] == 0, end, 0).astype(jnp.float32)
            usable = (row_index >= first_row) & (row_index < stop.astype(jnp.bfloat16))
            window = pl.ds(band * BAND_COLS, BAND_COLS)
            total[:, window] += jnp.where(usable, plane, zero).astype(jnp.float32)
            high[slot, :, window] = jnp.where(usable, plane, -sentinel)
            low[slot, :, window] = jnp.where(usable, plane, sentinel)

    def body(step, carry):
        @pl.when(step > 0)
        def _():
            body_copy(step).wait()

        held = first_pass(STRIDE * step)
        for i in range(STRIDE):
            ahead = first_pass(STRIDE * step + i + 1) if i + 1 < STRIDE else None
            second_pass(STRIDE * step + i, *held)
            held = ahead
        return carry

    lax.fori_loop(0, slots // STRIDE, body, 0)
    select_chunks(chunk_of, parts, high, low, total, outs)


def filter_slots(chunk_of, chunks, parts, exposures, pictures, halo, bank_v, bank_h, tables):
    slots, rows, columns = pictures.shape
    vmem = pl.BlockSpec(memory_space=pltpu.VMEM)
    return pl.pallas_call(
        functools.partial(filter_kernel, chunk_of, parts),
        out_shape=[
            jax.ShapeDtypeStruct(pictures.shape, jnp.bfloat16),
            jax.ShapeDtypeStruct(pictures.shape, jnp.bfloat16),
            jax.ShapeDtypeStruct(pictures.shape, jnp.bfloat16),
            jax.ShapeDtypeStruct((rows, columns), jnp.float32),
        ]
        + [jax.ShapeDtypeStruct((LISTS, TILE_ROWS, columns // parts), jnp.bfloat16)]
        * (chunks * parts),
        in_specs=[pl.BlockSpec(memory_space=pltpu.HBM)] + [vmem] * (4 + len(tables)),
        out_specs=[vmem] * (4 + chunks * parts),
        input_output_aliases={1: 0},
        scratch_shapes=[pltpu.SMEM(table.shape, table.dtype) for table in tables]
        + [
            pltpu.SemaphoreType.DMA((len(tables),)),
            pltpu.SemaphoreType.DMA((slots // STRIDE,)),
        ],
        compiler_params=pltpu.CompilerParams(vmem_limit_bytes=KERNEL_VMEM),
        cost_estimate=pl.CostEstimate(
            flops=4 * slots * rows * columns * 256, bytes_accessed=8 << 20, transcendentals=0
        ),
        name="filter_slots",
    )(
        pltpu.with_memory_space_constraint(exposures, pltpu.HBM),
        *[
            pltpu.with_memory_space_constraint(value, pltpu.VMEM)
            for value in (pictures, halo, bank_v, bank_h, *tables)
        ],
    )[1:]


def select_kernel(chunk_of, parts, high, low, total, *outs):
    select_chunks(chunk_of, parts, high, low, total, outs)


def select(chunk_of, chunks, parts, high, low, total):
    vmem = pl.BlockSpec(memory_space=pltpu.VMEM)
    return pl.pallas_call(
        functools.partial(select_kernel, chunk_of, parts),
        out_shape=[
            jax.ShapeDtypeStruct((LISTS, TILE_ROWS, high.shape[2] // parts), jnp.bfloat16)
        ]
        * (chunks * parts),
        in_specs=[vmem] * 3,
        out_specs=[vmem] * (chunks * parts),
        compiler_params=pltpu.CompilerParams(vmem_limit_bytes=KERNEL_VMEM),
        cost_estimate=pl.CostEstimate(flops=1 << 24, bytes_accessed=4 << 20, transcendentals=0),
        name="select_rows",
    )(*[pltpu.with_memory_space_constraint(value, pltpu.VMEM) for value in (high, low, total)])


def merged_lists(sources, ordered):
    sides = []
    for base, up in ((0, True), (REJECT, False)):
        lists = [[ref[base + i, :, window] for i in range(REJECT)] for ref, window in sources]
        while len(lists) > 1:
            keep = ordered or len(lists) > 2
            paired = [
                merged_four(lists[i], lists[i + 1], up, keep)
                for i in range(0, len(lists) - 1, 2)
            ]
            lists = paired + (lists[-1:] if len(lists) % 2 else [])
        sides.append(lists[0])
    grand = None
    for ref, window in sources:
        part = ref[2 * REJECT, :, window].astype(jnp.float32) + extremes_sum(
            [ref[i, :, window] for i in range(REJECT)],
            [ref[REJECT + i, :, window] for i in range(REJECT)],
        )
        grand = part if grand is None else grand + part
    return sides, grand


def merge_kernel(*refs):
    *sources, out = refs
    for band in range(out.shape[-1] // BAND_COLS):
        window = pl.ds(band * BAND_COLS, BAND_COLS)
        sides, grand = merged_lists([(ref, window) for ref in sources], True)
        for index, value in enumerate(sides[0] + sides[1]):
            out[index, :, window] = value
        out[2 * REJECT, :, window] = (grand - extremes_sum(*sides)).astype(jnp.bfloat16)


def merge(parts):
    vmem = pl.BlockSpec(memory_space=pltpu.VMEM)
    return pl.pallas_call(
        merge_kernel,
        out_shape=jax.ShapeDtypeStruct(parts[0].shape, jnp.bfloat16),
        in_specs=[vmem] * len(parts),
        out_specs=vmem,
        compiler_params=pltpu.CompilerParams(vmem_limit_bytes=KERNEL_VMEM),
        name="merge_lists",
    )(*parts)


def finish_kernel(exposures_total, whole, *refs):
    *sources, count_ref, coadd_ref, rejected_ref = refs
    whole, parts = sources[:whole], sources[whole:]
    for band in range(coadd_ref.shape[-1] // BAND_COLS):
        window = pl.ds(band * BAND_COLS, BAND_COLS)
        here = [(ref, window) for ref in whole]
        for index, ref in enumerate(parts):
            first, held = index * ref.shape[-1], ref.shape[-1]
            if first <= band * BAND_COLS < first + held:
                here.append((ref, pl.ds(band * BAND_COLS - first, BAND_COLS)))
        sides, grand = merged_lists(here, False)
        extremes = extremes_sum(*sides)
        count = count_ref[:, window]
        clipped = count >= MIN_VALID
        used = jnp.where(clipped, count - 2 * REJECT, count)
        kept = jnp.where(clipped, grand - extremes, grand)
        coadd_ref[:, window] = kept / jnp.maximum(used, 1).astype(jnp.float32)
        rejected_ref[:, window] = exposures_total - used


def finish(whole, parts, count, exposures_total):
    vmem = pl.BlockSpec(memory_space=pltpu.VMEM)
    return pl.pallas_call(
        functools.partial(finish_kernel, exposures_total, len(whole)),
        out_shape=[
            jax.ShapeDtypeStruct(count.shape, jnp.float32),
            jax.ShapeDtypeStruct(count.shape, jnp.int32),
        ],
        in_specs=[vmem] * (len(whole) + len(parts) + 1),
        out_specs=[vmem, vmem],
        compiler_params=pltpu.CompilerParams(vmem_limit_bytes=KERNEL_VMEM),
        name="finish_pixels",
    )(*whole, *parts, count)


def swapped(value, axis, distance):
    count = lax.axis_size(axis)
    return lax.ppermute(value, axis, [(i, i ^ distance) for i in range(count)])


def shards(
    exposures, slot_ids, row_range, bad_bands, kernel_choice, flux_scale, vert_taps, horiz_taps
):
    slot_count, row_dev, columns = exposures.shape
    exposures_total = flux_scale.shape[0]
    expo_size = lax.axis_size("expo")
    rows_out = row_dev // expo_size

    edges, bank_v = window_edges(exposures, vert_taps)
    halo = swapped(edges, "sky", 1)
    pictures, bank_h, count, *tables = prepare(
        rows_out,
        exposures,
        slot_ids,
        kernel_choice.T,
        bad_bands.T,
        row_range.T,
        flux_scale,
        horiz_taps,
    )

    if rows_out == TILE_ROWS and expo_size == 2 * SQUARE:
        high, low, total, far_z, far_both = filter_slots(
            lambda place, i: place ^ (i + 2) ^ SQUARE,
            SQUARE - 2,
            1,
            exposures,
            pictures,
            halo,
            bank_v,
            bank_h,
            tables,
        )
        got = [swapped(far_both, "expo", 3), swapped(far_z, "expo", 2)]
        far_y, kept = select(lambda place, i: place ^ (SQUARE + 1 - i), 2, 1, high, low, total)
        near = select(
            lambda place, i: place ^ i,
            SQUARE,
            1,
            high,
            low,
            total,
        )
        near = list(near)
        got.append(swapped(far_y, "expo", 1))
        near = near[:1] + [swapped(part, "expo", 1 + i) for i, part in enumerate(near[1:])]
        across = swapped(merge([kept] + got), "expo", SQUARE)
        coadd_plane, rejected_count = finish(
            [merge(near[:-1]), near[-1], across], [], count, exposures_total
        )
    else:
        chunks = row_dev // TILE_ROWS
        high, low, total, *lists = filter_slots(
            lambda place, i: i, chunks, 1, exposures, pictures, halo, bank_v, bank_h, tables
        )
        whole = jnp.concatenate(lists, 1)
        arrived = lax.all_to_all(whole, "expo", split_axis=1, concat_axis=0, tiled=True)
        arrived = arrived.reshape(expo_size, LISTS, rows_out, columns)
        coadd_plane, rejected_count = finish(
            [arrived[i] for i in range(expo_size)], [], count, exposures_total
        )
    return (coadd_plane[None], rejected_count[None])


def solution(mesh):
    in_specs = (
        P(("groups", "expo"), "sky", None),
        P("groups", None),
        P("groups", None),
        P("groups", None),
        P("groups", None),
        P("groups"),
        P("groups", None),
        P("groups", None),
    )
    out_specs = (P(("groups", "sky"), "expo", None), P(("groups", "sky"), "expo", None))
    return jax.shard_map(shards, mesh=mesh, in_specs=in_specs, out_specs=out_specs, check_vma=False)
```
